32 devices in a mesh: range: 16 (over z, y, core), pulse: 2 (over x).
Axes of the slice: x: 2, y: 2, z: 4, core: 2. Of those that a mesh axis runs over, the one named last changes fastest.
Arguments:
- echoes: float32 [2, 64, 2, 16384], P(None, None, 'pulse', 'range'), may hold values from -6 to 6
- steer_blocks: float32 [32, 2, 32, 8], P('pulse'), may hold values from -0.75 to 0.75
- plan: int32 [8, 4], replicated, may hold values from 0 to 7, as said below
- filter_taps: float32 [2, 1024], replicated, may hold values from -0.125 to 0.125
Outputs:
- compressed: float32 [2, 256, 2, 16384], P(None, 'pulse', None, 'range')
The draws below stay inside these ranges and needn't reach their ends.
Inputs may be any that keep to these rules, and one draw needn't show every extreme that they name: `plan`: each row names 4 different subarray blocks; rows 2m and 2m + 1 together name every subarray block once.
All inputs are finite; a program needn't handle non-finite values.
Results may differ from the reference program's by a relative error of at most 0.0001.
Values sent between devices are 32-bit elements; how exact they have to be, the bound alone decides.
No kernel may reach another device: no remote copies, remote signals or barrier semaphores. Data moves between devices by JAX's collectives and lax.ppermute only.
A program may use at most 128 MiB of HBM per device.

```python
import jax
import jax.numpy as jnp
from jax import lax

BEAMS = 256
SUBARRAYS = 64
TAPS = 1024
TILE = 128
BEAM_BLOCK = 32
SUB_BLOCK = 8
PER_BEAM = 4
PULSES = 2
GATES = 16384
BEAM_BLOCKS = 8
SUB_BLOCKS = 8
WEIGHT_BLOCKS = 32


def one_permutation(pair_key):
    return jax.random.permutation(pair_key, SUB_BLOCKS)


def draw_plan(key, part):
    pair_keys = jax.random.split(jax.random.fold_in(key, 7), BEAM_BLOCKS // 2)
    perms = jax.vmap(one_permutation)(pair_keys)
    return perms.reshape(BEAM_BLOCKS, PER_BEAM).astype(jnp.int32)


def shard_levels(key, dims, pieces, low, top_value):
    level, own = 1.0, jax.random.fold_in(key, 6)
    for dim, shards_of in pieces:
        draws = jnp.exp(jax.random.uniform(jax.random.fold_in(own, dim), (shards_of,), jnp.float32, low / len(pieces), top_value / len(pieces)))
        level = level * jnp.repeat(draws, dims[dim] // shards_of).reshape([-1 if axis == dim else 1 for axis in range(len(dims))])
    return level


def centred(own_key, shape, width, bound, cuts=(), held_as=jnp.bfloat16):
    result = jax.random.normal(own_key, shape, jnp.float32) * width
    if len(cuts) > 0:
        result = shard_levels(own_key, shape, cuts, -0.22, 0.18) * result
    return jnp.clip(result, min=-bound, max=bound).astype(held_as)


def setup_inputs(seed: int = 0) -> dict:
    streams_of = jax.random.split(jax.random.key(seed), 5)
    return {
        "echoes": centred(streams_of[0], (2, SUBARRAYS, PULSES, GATES), 1.0, 6.0, ((2, 2), (3, 16)), jnp.float32),
        "steer_blocks": centred(streams_of[1], (WEIGHT_BLOCKS, 2, BEAM_BLOCK, SUB_BLOCK), SUBARRAYS ** -0.5, 0.75, ((0, 2),), jnp.float32),
        "plan": draw_plan(jax.random.fold_in(streams_of[4], 71), 0),
        "filter_taps": centred(streams_of[3], (2, TAPS), (2 * TAPS) ** -0.5, 0.125, (), jnp.float32),
    }


highest = lax.Precision.HIGHEST


def steering_matrix(blocks, sched_rows):
    count = sched_rows.shape[0]
    per_beam = sched_rows.shape[1]
    one_hot = (sched_rows[:, :, None] == jnp.arange(SUB_BLOCKS, dtype=jnp.int32)[None, None, :]).astype(jnp.float32)
    shaped = blocks.reshape(count, per_beam, 2, blocks.shape[2], blocks.shape[3])
    dense = jnp.einsum("ikc,ikzbs->zibcs", one_hot, shaped, precision=highest)
    return dense.reshape(2, count * blocks.shape[2], SUB_BLOCKS * blocks.shape[3])


def form_beams(weights, echo_part):
    flat = echo_part.reshape(2, echo_part.shape[1], echo_part.shape[2] * echo_part.shape[3])
    real_part = jnp.dot(weights[0], flat[0], precision=highest, preferred_element_type=jnp.float32) - jnp.dot(weights[1], flat[1], precision=highest, preferred_element_type=jnp.float32)
    imag_part = jnp.dot(weights[0], flat[1], precision=highest, preferred_element_type=jnp.float32) + jnp.dot(weights[1], flat[0], precision=highest, preferred_element_type=jnp.float32)
    return jnp.stack([real_part, imag_part]).reshape(2, weights.shape[1], echo_part.shape[2], echo_part.shape[3])


def toeplitz_tables(filter_taps):
    taps_len = filter_taps.shape[1]
    span = taps_len // TILE
    padded = jnp.concatenate([filter_taps, jnp.zeros((2, TILE + 1), filter_taps.dtype)], axis=1)
    length = taps_len + TILE + 1
    repeated = jnp.tile(padded, (1, TILE))[:, :TILE * (length - 1)]
    skewed = repeated.reshape(2, TILE, length - 1)
    return skewed.reshape(2, TILE, span + 1, TILE).transpose(0, 2, 1, 3)


def real_tile(source, table):
    return jnp.einsum("rjm,mn->rjn", source, table, precision=highest, preferred_element_type=jnp.float32)


def complex_tile(source, table):
    real_part = real_tile(source[0], table[0]) - real_tile(source[1], table[1])
    imag_part = real_tile(source[0], table[1]) + real_tile(source[1], table[0])
    return jnp.stack([real_part, imag_part])


def whole_compress(beam_out, tables):
    row_count = beam_out.shape[1] * beam_out.shape[2]
    out_blocks = beam_out.shape[3] // TILE
    span = tables.shape[1] - 1
    local = beam_out.reshape(2, row_count, out_blocks, TILE)
    extended = jnp.concatenate([jnp.zeros((2, row_count, span, TILE), jnp.float32), local], axis=2)
    running = jnp.zeros((2, row_count, out_blocks, TILE), jnp.float32)
    for offset in range(span + 1):
        running = running + complex_tile(extended[:, :, span - offset:span - offset + out_blocks], tables[:, offset])
    return running.reshape(beam_out.shape)


def reference(echoes, steer_blocks, plan, filter_taps):
    weights = steering_matrix(steer_blocks, plan)
    tables = toeplitz_tables(filter_taps)
    grouped = weights.reshape(2, BEAM_BLOCKS, BEAM_BLOCK, SUBARRAYS).transpose(1, 0, 2, 3)

    def one_group(group_weights):
        return whole_compress(form_beams(group_weights, echoes), tables)

    stacked = lax.map(one_group, grouped)
    return stacked.transpose(1, 0, 2, 3, 4).reshape(2, BEAMS, PULSES, GATES)
```

```python
import functools

import jax
import jax.numpy as jnp
from jax import lax
from jax.experimental import pallas as pl
from jax.experimental.pallas import tpu as pltpu
from jax.sharding import PartitionSpec as P

TILE = 128
f32 = jnp.float32
bf16 = jnp.bfloat16
VMEM = pl.BlockSpec(memory_space=pltpu.VMEM)
SMEM = pl.BlockSpec(memory_space=pltpu.SMEM)


def dot(left, right):
    return jnp.dot(left, right, preferred_element_type=f32)


def split(value):
    high = value.astype(bf16)
    return high, (value - high.astype(f32)).astype(bf16)


def shifted(value, axis, steps):
    count = lax.axis_size(axis)
    return lax.ppermute(value, axis, [(i, (i + steps) % count) for i in range(count)])


def table_kernel(taps_ref, high_ref, low_ref):
    span = taps_ref.shape[1] // TILE
    row = lax.broadcasted_iota(jnp.int32, (TILE, TILE), 0)
    lane = lax.broadcasted_iota(jnp.int32, (TILE, TILE), 1)
    upper = lane >= row
    before = [jnp.zeros((TILE, TILE), f32)] * 2
    for offset in range(span + 1):
        for part in range(2):
            if offset < span:
                taps = taps_ref[part : part + 1, offset * TILE : (offset + 1) * TILE]
                rolled = pltpu.roll(
                    jnp.broadcast_to(taps, (TILE, TILE)), 0, 1, stride=1, stride_axis=0
                )
            else:
                rolled = jnp.zeros((TILE, TILE), f32)
            table = jnp.where(upper, rolled, before[part])
            before[part] = rolled
            high, low = split(table)
            for ref, value in ((high_ref, high), (low_ref, low)):
                if part == 0:
                    ref[offset, :TILE, :TILE] = value
                    ref[offset, TILE:, TILE:] = value
                else:
                    ref[offset, :TILE, TILE:] = value
                    ref[offset, TILE:, :TILE] = -value


def filter_tables(filter_taps):
    span = filter_taps.shape[1] // TILE
    shape = jax.ShapeDtypeStruct((span + 1, 2 * TILE, 2 * TILE), bf16)
    return pl.pallas_call(
        table_kernel,
        out_shape=(shape, shape),
        in_specs=[VMEM],
        out_specs=(VMEM, VMEM),
        name="tables",
        compiler_params=pltpu.CompilerParams(vmem_limit_bytes=16 << 20),
        cost_estimate=pl.CostEstimate(flops=1 << 20, bytes_accessed=2 << 20, transcendentals=0),
    )(filter_taps)


def weight_kernel(groups, plan_ref, steer_ref, high_ref, low_ref, wide):
    beam_blocks = steer_ref.shape[0] // plan_ref.shape[1]
    per_beam = plan_ref.shape[1]
    sub = steer_ref.shape[2]
    width = steer_ref.shape[3]
    beams = beam_blocks * width
    first = lax.axis_index("pulse") * beam_blocks
    wide[...] = jnp.zeros_like(wide)
    cut = groups[0]
    total = groups[0] + groups[1]
    for i in range(beam_blocks):
        for k in range(per_beam):
            start = plan_ref[first + i, k] * sub
            in_first = start < cut
            size = jnp.where(in_first, groups[0], groups[1])
            base = jnp.where(in_first, start, start + cut)
            re_row = pl.multiple_of(base, sub)
            im_row = pl.multiple_of(base + size, sub)
            real = steer_ref[i * per_beam + k, 0]
            imag = steer_ref[i * per_beam + k, 1]
            left = slice(i * width, (i + 1) * width)
            right = slice(beams + i * width, beams + (i + 1) * width)
            wide[pl.ds(re_row, sub), left] = real
            wide[pl.ds(im_row, sub), left] = -imag
            wide[pl.ds(re_row, sub), right] = imag
            wide[pl.ds(im_row, sub), right] = real
    high, low = split(wide[...].T)
    high_ref[...] = high
    low_ref[...] = low


def steering(plan, steer_blocks, groups):
    beams = steer_blocks.shape[0] // plan.shape[1] * steer_blocks.shape[2]
    depth = 2 * sum(groups)
    shape = jax.ShapeDtypeStruct((2 * beams, depth), bf16)
    return pl.pallas_call(
        functools.partial(weight_kernel, groups),
        out_shape=(shape, shape),
        in_specs=[SMEM, VMEM],
        out_specs=(VMEM, VMEM),
        scratch_shapes=[pltpu.VMEM((depth, 2 * beams), f32)],
        name="steering",
        compiler_params=pltpu.CompilerParams(vmem_limit_bytes=16 << 20),
        cost_estimate=pl.CostEstimate(flops=1 << 18, bytes_accessed=1 << 18, transcendentals=0),
    )(plan, steer_blocks.transpose(0, 1, 3, 2))


def filter_kernel(before_ref, own_ref, high_ref, low_ref, out_ref, xh, xl):
    rows, blocks = own_ref.shape[1:3]
    span = before_ref.shape[2]
    first = lax.axis_index("range") == 0
    for block in range(span + blocks):
        for part in range(2):
            if block < span:
                value = jnp.where(first, 0.0, before_ref[part, :, block, :])
            else:
                value = own_ref[part, :, block - span, :]
            high, low = split(value)
            at = (slice(block * rows, (block + 1) * rows), slice(part * TILE, (part + 1) * TILE))
            xh[at] = high
            xl[at] = low
    total = None
    for offset in range(span + 1):
        at = slice((span - offset) * rows, (span - offset + blocks) * rows)
        term = dot(xh[at, :], high_ref[offset]) + dot(xl[at, :], high_ref[offset])
        term = term + dot(xh[at, :], low_ref[offset])
        total = term if total is None else total + term
    out_ref[...] = total


def filtered(before, own, tables):
    rows, blocks = own.shape[1:3]
    span = before.shape[2]
    return pl.pallas_call(
        filter_kernel,
        out_shape=jax.ShapeDtypeStruct((blocks * rows, 2 * TILE), f32),
        in_specs=[VMEM] * 4,
        out_specs=VMEM,
        scratch_shapes=[pltpu.VMEM(((span + blocks) * rows, 2 * TILE), bf16)] * 2,
        name="filter",
        compiler_params=pltpu.CompilerParams(vmem_limit_bytes=16 << 20),
        cost_estimate=pl.CostEstimate(
            flops=6 * (span + 1) * blocks * rows * 4 * TILE * TILE,
            bytes_accessed=3 << 20,
            transcendentals=0,
        ),
    )(before, own, *tables)


def beam_kernel(pulses, high_ref, low_ref, *rest):
    y_refs, out_ref, yh, yl = rest[: 2 * pulses], *rest[2 * pulses :]
    beams = high_ref.shape[0] // 2
    blocks = yh.shape[2] // TILE
    mine = lax.axis_index("pulse")
    for shift in range(pulses):
        pulse = lax.rem(mine - shift + pulses, pulses)
        base = 0
        for ref in y_refs[2 * shift : 2 * shift + 2]:
            rows = ref.shape[0] // blocks
            for block in range(blocks):
                for part in range(2):
                    high, low = split(
                        ref[block * rows : (block + 1) * rows, part * TILE : (part + 1) * TILE]
                    )
                    at = (
                        pulse,
                        slice(base + part * rows, base + (part + 1) * rows),
                        slice(block * TILE, (block + 1) * TILE),
                    )
                    yh[at] = high
                    yl[at] = low
            base += 2 * rows
    stride = blocks * pulses
    for pulse in range(pulses):
        for block in range(0, blocks, 2):
            lanes = slice(block * TILE, (block + 2) * TILE)
            out = dot(high_ref[...], yh[pulse, :, lanes])
            out = out + dot(low_ref[...], yh[pulse, :, lanes])
            out = out + dot(high_ref[...], yl[pulse, :, lanes])
            for part in range(2):
                for beam in range(0, beams, 8):
                    row = part * beams + beam
                    for half in range(2):
                        start = beam * stride + (block + half) * pulses + pulse
                        out_ref[part, pl.ds(start, 8, stride=stride), :] = out[
                            row : row + 8, half * TILE : (half + 1) * TILE
                        ]


def formed(weights, pairs, blocks):
    pulses = len(pairs)
    beams, depth = weights[0].shape[0] // 2, weights[0].shape[1]
    gates = blocks * TILE
    out = pl.pallas_call(
        functools.partial(beam_kernel, pulses),
        out_shape=jax.ShapeDtypeStruct((2, beams * blocks * pulses, TILE), f32),
        in_specs=[VMEM] * (2 + 2 * pulses),
        out_specs=VMEM,
        scratch_shapes=[pltpu.VMEM((pulses, depth, gates), bf16)] * 2,
        name="beams",
        compiler_params=pltpu.CompilerParams(vmem_limit_bytes=24 << 20),
        cost_estimate=pl.CostEstimate(
            flops=6 * pulses * 2 * beams * depth * gates,
            bytes_accessed=4 << 20,
            transcendentals=0,
        ),
    )(*weights, *[y for pair in pairs for y in pair])
    out = out.reshape(2, beams, blocks, pulses, TILE).transpose(0, 1, 3, 2, 4)
    return out.reshape(2, beams, pulses, gates)


def body(echoes, steer_blocks, plan, filter_taps):
    pulses = lax.axis_size("pulse")
    subarrays, gates = echoes.shape[1], echoes.shape[3]
    blocks = gates // TILE
    span = filter_taps.shape[1] // TILE
    assert echoes.shape[2] == 1 and blocks >= span
    cut = subarrays // 2
    groups = (cut, subarrays - cut)
    samples = echoes.reshape(2, subarrays, blocks, TILE)
    raw, rest = samples[:, :cut], samples[:, cut:]
    others_raw = [shifted(raw, "pulse", k) for k in range(1, pulses)]
    before_rest = shifted(rest[:, :, blocks - span :], "range", 1)
    before_raw = shifted(raw[:, :, blocks - span :], "range", 1)
    tables = filter_tables(filter_taps)
    weights = steering(plan, steer_blocks, groups)
    own_rest = filtered(before_rest, rest, tables)
    others_rest = [shifted(own_rest, "pulse", k) for k in range(1, pulses)]
    own_raw = filtered(before_raw, raw, tables)
    before_others = [shifted(r[:, :, blocks - span :], "range", 1) for r in others_raw]
    filtered_others = [filtered(b, r, tables) for b, r in zip(before_others, others_raw)]
    pairs = [(own_raw, own_rest)] + list(zip(filtered_others, others_rest))
    return formed(weights, pairs, blocks)


def solution(mesh):
    in_specs = (P(None, None, "pulse", "range"), P("pulse", None, None, None), P(), P())
    out_specs = P(None, "pulse", None, "range")
    return jax.shard_map(body, mesh=mesh, in_specs=in_specs, out_specs=out_specs, check_vma=False)
```

```python
import functools

import jax
import jax.numpy as jnp
from jax import lax
from jax.experimental import pallas as pl
from jax.experimental.pallas import tpu as pltpu
from jax.sharding import PartitionSpec as P

TILE = 128
f32 = jnp.float32
bf16 = jnp.bfloat16
VMEM = pl.BlockSpec(memory_space=pltpu.VMEM)
SMEM = pl.BlockSpec(memory_space=pltpu.SMEM)


def dot(left, right):
    return jnp.dot(left, right, preferred_element_type=f32)


def split(value):
    high = value.astype(bf16)
    return high, (value - high.astype(f32)).astype(bf16)


def shifted(value, axis, steps):
    count = lax.axis_size(axis)
    return lax.ppermute(value, axis, [(i, (i + steps) % count) for i in range(count)])


def from_odd(value):
    count = lax.axis_size("range")
    target = {i: (i + 1) % count for i in range(count)}
    source, goal = count - 1, count - 5
    while goal > 0:
        target[source] = goal
        source, goal = goal - 1, goal - 4
    target[source] = 0
    return lax.ppermute(value, "range", list(target.items()))


def from_even(value):
    count = lax.axis_size("range")
    return lax.ppermute(value, "range", [(i, i ^ 1) for i in range(count)])


def make_tables(taps_ref, high_ref, low_ref):
    span = taps_ref.shape[1] // TILE
    row = lax.broadcasted_iota(jnp.int32, (TILE, TILE), 0)
    lane = lax.broadcasted_iota(jnp.int32, (TILE, TILE), 1)
    upper = lane >= row
    before = [jnp.zeros((TILE, TILE), f32)] * 2
    for offset in range(span + 1):
        for part in range(2):
            if offset < span:
                taps = taps_ref[part : part + 1, offset * TILE : (offset + 1) * TILE]
                rolled = pltpu.roll(
                    jnp.broadcast_to(taps, (TILE, TILE)), 0, 1, stride=1, stride_axis=0
                )
            else:
                rolled = jnp.zeros((TILE, TILE), f32)
            table = jnp.where(upper, rolled, before[part])
            before[part] = rolled
            high, low = split(table)
            for ref, value in ((high_ref, high), (low_ref, low)):
                if part == 0:
                    ref[offset, :TILE, :TILE] = value
                    ref[offset, TILE:, TILE:] = value
                else:
                    ref[offset, :TILE, TILE:] = value
                    ref[offset, TILE:, :TILE] = -value


def make_weights(plan_ref, steer_ref, high_ref, low_ref, wide, cut):
    per_beam = plan_ref.shape[0]
    sub, width = steer_ref.shape[2:]
    beam_blocks = steer_ref.shape[0] // per_beam
    beams = beam_blocks * width
    total = wide.shape[0] // 2
    first = lax.axis_index("pulse") * beam_blocks
    column = lax.broadcasted_iota(jnp.int32, plan_ref.shape, 1)
    for i in range(beam_blocks):
        mine = jnp.sum(jnp.where(column == first + i, plan_ref[...], 0), axis=1, keepdims=True)
        chosen = [mine[k : k + 1] for k in range(per_beam)]
        left = slice(i * width, (i + 1) * width)
        right = slice(beams + i * width, beams + (i + 1) * width)
        for block in range(total // sub):
            real = imag = jnp.zeros((sub, width), f32)
            for k in range(per_beam):
                here = jnp.broadcast_to(chosen[k] == block, (sub, width))
                real = jnp.where(here, steer_ref[i * per_beam + k, 0], real)
                imag = jnp.where(here, steer_ref[i * per_beam + k, 1], imag)
            start = block * sub
            if start < cut:
                re_row, im_row = start, start + cut
            else:
                re_row, im_row = start + cut, start + total
            wide[re_row : re_row + sub, left] = real
            wide[im_row : im_row + sub, left] = -imag
            wide[re_row : re_row + sub, right] = imag
            wide[im_row : im_row + sub, right] = real
    high, low = split(wide[...].T)
    high_ref[...] = high
    low_ref[...] = low


def place(value, block, part, xh, xl):
    rows = value.shape[0]
    high, low = split(value)
    at = (slice(block * rows, (block + 1) * rows), slice(part * TILE, (part + 1) * TILE))
    xh[at] = high
    xl[at] = low


def product(xh, xl, at, high, low):
    return dot(xh[at, :], high) + dot(xl[at, :], high) + dot(xh[at, :], low)


def inner(own_ref, high_ref, low_ref, out_ref, xh, xl):
    rows, blocks = own_ref.shape[1:3]
    span = high_ref.shape[0] - 1
    for part in range(2):
        value = jnp.swapaxes(own_ref[part], 0, 1)
        for block in range(blocks):
            place(value[block], block, part, xh, xl)
    at = slice(0, blocks * rows)
    out_ref[...] = product(xh, xl, at, high_ref[0], low_ref[0])
    for offset in range(1, min(span + 1, blocks)):
        at = slice(0, (blocks - offset) * rows)
        out_ref[offset * rows :, :] += product(xh, xl, at, high_ref[offset], low_ref[offset])


def outer(even_ref, first_row, odd_ref, high_ref, low_ref, out_ref, xh, xl):
    rows, span = odd_ref.shape[1:3]
    index = lax.axis_index("range")
    odd = lax.rem(index, 2) == 1
    for part in range(2):
        value = jnp.where(odd, even_ref[part, first_row : first_row + rows], odd_ref[part])
        value = jnp.swapaxes(jnp.where(index == 0, 0.0, value), 0, 1)
        for block in range(span):
            place(value[block], block, part, xh, xl)
    for offset in range(1, span + 1):
        at = slice((span - offset) * rows, span * rows)
        out_ref[: offset * rows, :] += product(xh, xl, at, high_ref[offset], low_ref[offset])


def columns(ref, blocks, yh, yl):
    rows = ref.shape[0] // blocks
    for block in range(blocks):
        lanes = slice(block * TILE, (block + 1) * TILE)
        for part in range(2):
            value = ref[block * rows : (block + 1) * rows, part * TILE : (part + 1) * TILE]
            high, low = split(value)
            yh[part * rows : (part + 1) * rows, lanes] = high
            yl[part * rows : (part + 1) * rows, lanes] = low


def share(wh, wl, at, yh, yl, lanes):
    left = jnp.concatenate([wh[:, at], wh[:, at], wl[:, at]], axis=1)
    right = jnp.concatenate([yh[:, lanes], yl[:, lanes], yh[:, lanes]], axis=0)
    return dot(left, right)


def send(shift, dense, out_ref, start, stop, sems):
    count = dense.shape[0] // 2
    pulses = out_ref.shape[3]
    pulse = lax.rem(lax.axis_index("pulse") + pulses - shift, pulses)
    copies = []
    for block in range(start, stop):
        for part in range(2):
            copy = pltpu.make_async_copy(
                dense.at[part * count : (part + 1) * count, block * TILE : (block + 1) * TILE],
                out_ref.at[part, :, block, pulse, :],
                sems.at[2 * block + part],
            )
            copy.start()
            copies.append(copy)
    return copies


def prepare_kernel(taps, rest, th, tl, partial, xh, xl):
    make_tables(taps, th, tl)
    inner(rest, th, tl, partial, xh, xl)


def rest_kernel(cut, even, odd, partial, th, tl, out, xh, xl):
    out[...] = partial[...]
    outer(even, cut, odd, th, tl, out, xh, xl)


def own_kernel(others, plan, steer, even, odd, own, rest, th, tl, *refs):
    raws, (out, wh, wl), partials = refs[:others], refs[others : others + 3], refs[others + 3 : 2 * others + 3]
    first, xh, xl, ah, al, bh, bl, dense, sems, wide = refs[2 * others + 3 :]
    blocks = out.shape[2]
    cut = own.shape[1]
    make_weights(plan, steer, wh, wl, wide, cut)
    columns(rest, blocks, bh, bl)
    inner(own, th, tl, first, xh, xl)
    outer(even, 0, odd, th, tl, first, xh, xl)
    columns(first, blocks, ah, al)
    copies = []
    for block in range(0, blocks, 2):
        lanes = slice(block * TILE, (block + 2) * TILE)
        dense[:, lanes] = share(wh, wl, slice(0, 2 * cut), ah, al, lanes)
        dense[:, lanes] += share(wh, wl, slice(2 * cut, None), bh, bl, lanes)
        copies += send(0, dense, out, block, block + 2, sems)
    for raw, partial in zip(raws, partials):
        inner(raw, th, tl, partial, xh, xl)
    for copy in copies:
        copy.wait()


def share_kernel(cut, blocks, rest, wh, wl, out, bh, bl):
    columns(rest, blocks, bh, bl)
    for block in range(0, blocks, 2):
        lanes = slice(block * TILE, (block + 2) * TILE)
        out[:, lanes] = share(wh, wl, slice(2 * cut, None), bh, bl, lanes)


def other_kernel(shift, part, odd, even, partial, th, tl, wh, wl, held, out, *refs):
    first, xh, xl, ah, al, dense, sems = refs
    blocks = out.shape[2]
    first[...] = partial[...]
    outer(even, 0, odd, th, tl, first, xh, xl)
    columns(first, blocks, ah, al)
    copies = []
    for block in range(0, blocks, 2):
        lanes = slice(block * TILE, (block + 2) * TILE)
        dense[:, lanes] = share(wh, wl, slice(0, ah.shape[0]), ah, al, lanes) + part[:, lanes]
        copies += send(shift, dense, out, block, block + 2, sems)
    for copy in copies:
        copy.wait()


def call(kernel, name, out_shape, in_specs, out_specs, scratch_shapes, flops=1000, **kwargs):
    return pl.pallas_call(
        kernel,
        out_shape=out_shape,
        in_specs=in_specs,
        out_specs=out_specs,
        scratch_shapes=scratch_shapes,
        name=name,
        compiler_params=pltpu.CompilerParams(vmem_limit_bytes=16 << 20),
        cost_estimate=pl.CostEstimate(flops=flops, bytes_accessed=1000, transcendentals=0),
        **kwargs,
    )


def body(echoes, steer_blocks, plan, filter_taps):
    pulses = lax.axis_size("pulse")
    subarrays, gates = echoes.shape[1], echoes.shape[3]
    blocks = gates // TILE
    span = filter_taps.shape[1] // TILE
    assert echoes.shape[2] == 1 and blocks >= span and lax.axis_size("range") % 4 == 0
    cut = subarrays // 2
    left = subarrays - cut
    depth = 2 * subarrays
    count = steer_blocks.shape[0] // plan.shape[1] * steer_blocks.shape[2]
    any_space = pl.BlockSpec(memory_space=pl.ANY)

    def shape(*dims, dtype=f32):
        return jax.ShapeDtypeStruct(dims, dtype)

    def halves(rows):
        return [pltpu.VMEM((blocks * rows, 2 * TILE), bf16)] * 2

    def columns_of(rows):
        return [pltpu.VMEM((2 * rows, gates), bf16)] * 2

    out_shape = shape(2, count, blocks, pulses, TILE)
    dense = [pltpu.VMEM((2 * count, gates), f32), pltpu.SemaphoreType.DMA((2 * blocks,))]

    samples = echoes.reshape(2, subarrays, blocks, TILE)
    tail = slice(blocks - span, blocks)
    raw, rest = samples[:, :cut], samples[:, cut:]
    odd_rest = from_odd(rest[:, :, tail])
    others_raw = [shifted(raw, "pulse", k) for k in range(1, pulses)]
    even = from_even(samples[:, :, tail])
    odd_raw = from_odd(raw[:, :, tail])

    *tables, partial_rest = call(
        prepare_kernel,
        "prepare",
        [shape(span + 1, 2 * TILE, 2 * TILE, dtype=bf16)] * 2 + [shape(blocks * left, 2 * TILE)],
        [VMEM] * 2,
        [VMEM] * 3,
        halves(left),
    )(filter_taps, rest)
    own_rest = call(
        functools.partial(rest_kernel, cut),
        "rest",
        shape(blocks * left, 2 * TILE),
        [VMEM] * 5,
        VMEM,
        halves(left),
    )(even, odd_rest, partial_rest, *tables)
    others_rest = [shifted(own_rest, "pulse", k) for k in range(1, pulses)]
    others_raw, own_rest = lax.optimization_barrier((others_raw, own_rest))
    odd_others = [from_odd(r[:, :, tail]) for r in others_raw]
    even_others = [from_even(r[:, :, tail]) for r in others_raw]
    out, *made = call(
        functools.partial(own_kernel, pulses - 1),
        "own",
        [out_shape]
        + [shape(2 * count, depth, dtype=bf16)] * 2
        + [shape(blocks * cut, 2 * TILE)] * (pulses - 1),
        [VMEM] * (7 + pulses),
        [any_space] + [VMEM] * (1 + pulses),
        [
            pltpu.VMEM((blocks * cut, 2 * TILE), f32),
            *halves(cut),
            *columns_of(cut),
            *columns_of(left),
            *dense,
            pltpu.VMEM((depth, 2 * count), f32),
        ],
    )(plan.T, steer_blocks.transpose(0, 1, 3, 2), even, odd_raw, raw, own_rest, *tables, *others_raw)
    weights, partials = made[:2], made[2:]
    for k in range(1, pulses):
        part = call(
            functools.partial(share_kernel, cut, blocks),
            "share",
            shape(2 * count, gates),
            [VMEM] * 3,
            VMEM,
            columns_of(left),
            flops=1 << 36,
        )(others_rest[k - 1], *weights)
        out = call(
            functools.partial(other_kernel, k),
            "other",
            out_shape,
            [VMEM] * 8 + [any_space],
            any_space,
            [pltpu.VMEM((blocks * cut, 2 * TILE), f32), *halves(cut), *columns_of(cut), *dense],
            input_output_aliases={8: 0},
        )(part, odd_others[k - 1], even_others[k - 1], partials[k - 1], *tables, *weights, out)
    return out.transpose(0, 1, 3, 2, 4).reshape(2, count, pulses, gates)


def solution(mesh):
    in_specs = (P(None, None, "pulse", "range"), P("pulse", None, None, None), P(), P())
    out_specs = P(None, "pulse", None, "range")
    return jax.shard_map(body, mesh=mesh, in_specs=in_specs, out_specs=out_specs, check_vma=False)
```

```python
import functools

import jax
import jax.numpy as jnp
from jax import lax
from jax.experimental import pallas as pl
from jax.experimental.pallas import tpu as pltpu
from jax.sharding import PartitionSpec as P

TILE = 128
f32 = jnp.float32
bf16 = jnp.bfloat16
VMEM = pl.BlockSpec(memory_space=pltpu.VMEM)
SMEM = pl.BlockSpec(memory_space=pltpu.SMEM)


def dot(left, right):
    return jnp.dot(left, right, preferred_element_type=f32)


def split(value):
    high = value.astype(bf16)
    return high, (value - high.astype(f32)).astype(bf16)


def shifted(value, axis, steps):
    count = lax.axis_size(axis)
    return lax.ppermute(value, axis, [(i, (i + steps) % count) for i in range(count)])


def from_odd(value):
    count = lax.axis_size("range")
    target = {i: (i + 1) % count for i in range(count)}
    source, goal = count - 1, count - 5
    while goal > 0:
        target[source] = goal
        source, goal = goal - 1, goal - 4
    target[source] = 0
    return lax.ppermute(value, "range", list(target.items()))


def from_even(value):
    count = lax.axis_size("range")
    return lax.ppermute(value, "range", [(i, i ^ 1) for i in range(count)])


def make_tables(taps_ref, high_ref, low_ref):
    span = taps_ref.shape[1] // TILE
    row = lax.broadcasted_iota(jnp.int32, (TILE, TILE), 0)
    lane = lax.broadcasted_iota(jnp.int32, (TILE, TILE), 1)
    upper = lane >= row
    before = [jnp.zeros((TILE, TILE), f32)] * 2
    for offset in range(span + 1):
        for part in range(2):
            if offset < span:
                taps = taps_ref[part : part + 1, offset * TILE : (offset + 1) * TILE]
                rolled = pltpu.roll(
                    jnp.broadcast_to(taps, (TILE, TILE)), 0, 1, stride=1, stride_axis=0
                )
            else:
                rolled = jnp.zeros((TILE, TILE), f32)
            table = jnp.where(upper, rolled, before[part])
            before[part] = rolled
            high, low = split(table)
            for ref, value in ((high_ref, high), (low_ref, low)):
                if part == 0:
                    ref[offset, :TILE, :TILE] = value
                    ref[offset, TILE:, TILE:] = value
                else:
                    ref[offset, :TILE, TILE:] = value
                    ref[offset, TILE:, :TILE] = -value


def make_weights(plan_ref, steer_ref, outs, wide, groups):
    per_beam = plan_ref.shape[0]
    sub, width = steer_ref.shape[2:]
    beam_blocks = steer_ref.shape[0] // per_beam
    beams = beam_blocks * width
    first = lax.axis_index("pulse") * beam_blocks
    column = lax.broadcasted_iota(jnp.int32, plan_ref.shape, 1)
    for i in range(beam_blocks):
        mine = jnp.sum(jnp.where(column == first + i, plan_ref[...], 0), axis=1, keepdims=True)
        chosen = [mine[k : k + 1] for k in range(per_beam)]
        left = slice(i * width, (i + 1) * width)
        right = slice(beams + i * width, beams + (i + 1) * width)
        for at, size in groups:
            for start in range(at, at + size, sub):
                real = imag = jnp.zeros((sub, width), f32)
                for k in range(per_beam):
                    here = jnp.broadcast_to(chosen[k] == start // sub, (sub, width))
                    real = jnp.where(here, steer_ref[i * per_beam + k, 0], real)
                    imag = jnp.where(here, steer_ref[i * per_beam + k, 1], imag)
                re_row = at + start
                im_row = re_row + size
                wide[re_row : re_row + sub, left] = real
                wide[im_row : im_row + sub, left] = -imag
                wide[re_row : re_row + sub, right] = imag
                wide[im_row : im_row + sub, right] = real
    for ref, (at, size) in zip(outs, groups):
        high, low = split(wide[2 * at : 2 * (at + size), :].T)
        ref[...] = jnp.concatenate([high, high, low], axis=1)


def place(value, xh, xl, part):
    blocks, rows = value.shape[:2]
    for block in range(blocks):
        high, low = split(value[block])
        at = (slice(block * rows, (block + 1) * rows), slice(part * TILE, (part + 1) * TILE))
        xh[at] = high
        xl[at] = low


def product(xh, xl, at, high, low):
    return dot(xh[at, :], high) + dot(xl[at, :], high) + dot(xh[at, :], low)


def inner(own_ref, high_ref, low_ref, out_ref, xh, xl):
    rows, blocks = own_ref.shape[1:3]
    span = high_ref.shape[0] - 1
    for part in range(2):
        place(jnp.swapaxes(own_ref[part], 0, 1), xh, xl, part)
    at = slice(0, blocks * rows)
    out_ref[...] = product(xh, xl, at, high_ref[0], low_ref[0])
    for offset in range(1, min(span + 1, blocks)):
        at = slice(0, (blocks - offset) * rows)
        out_ref[offset * rows :, :] += product(xh, xl, at, high_ref[offset], low_ref[offset])


def spill(high_ref, low_ref, out_ref, xh, xl):
    span = high_ref.shape[0] - 1
    rows = xh.shape[0] // span
    for offset in range(1, span + 1):
        at = slice((span - offset) * rows, span * rows)
        out_ref[: offset * rows, :] += product(xh, xl, at, high_ref[offset], low_ref[offset])


def outer(even_ref, start, odd_ref, high_ref, low_ref, out_ref, xh, xl):
    rows, span = odd_ref.shape[1:3]
    index = lax.axis_index("range")
    odd = lax.rem(index, 2) == 1
    for part in range(2):
        value = jnp.where(odd, even_ref[part, start : start + rows], odd_ref[part])
        place(jnp.swapaxes(jnp.where(index == 0, 0.0, value), 0, 1), xh, xl, part)
    spill(high_ref, low_ref, out_ref, xh, xl)


def columns(ref, y):
    blocks = y.shape[1] // TILE
    rows = y.shape[0] // 6
    for block in range(blocks):
        lanes = slice(block * TILE, (block + 1) * TILE)
        for part in range(2):
            high, low = split(ref[block * rows : (block + 1) * rows, part * TILE : (part + 1) * TILE])
            for copy, value in enumerate((high, low, high)):
                base = (2 * copy + part) * rows
                y[base : base + rows, lanes] = value


def send(shift, dense, out_ref, start, stop, sems):
    count = dense.shape[0] // 2
    pulses = out_ref.shape[3]
    pulse = lax.rem(lax.axis_index("pulse") + pulses - shift, pulses)
    copies = []
    for block in range(start, stop):
        for part in range(2):
            copy = pltpu.make_async_copy(
                dense.at[part * count : (part + 1) * count, block * TILE : (block + 1) * TILE],
                out_ref.at[part, :, block, pulse, :],
                sems.at[2 * block + part],
            )
            copy.start()
            copies.append(copy)
    return copies


def parts_of(blocks):
    half = -(-blocks // 2)
    return [(0, half), (half, blocks)] if half < blocks else [(0, blocks)]


def prepare_kernel(taps, raw, rest, th, tl, raw_partial, rest_partial, *scratch):
    make_tables(taps, th, tl)
    inner(rest, th, tl, rest_partial, *scratch[:2])
    inner(raw, th, tl, raw_partial, *scratch[2:])


def rest_kernel(cut, even, odd, partial, th, tl, out, xh, xl):
    rows = partial.shape[0]
    out[:rows, :] = partial[...]
    out[rows:, :] = jnp.zeros((out.shape[0] - rows, out.shape[1]), f32)
    outer(even, cut, odd, th, tl, out, xh, xl)


def own_kernel(groups, others, plan, steer, even, odd, partial, rest, th, tl, *refs):
    raws, (out, wa, wb), partials = refs[:others], refs[others : others + 3], refs[others + 3 : 2 * others + 3]
    first, xh, xl, ya, yb, dense, sems, wide = refs[2 * others + 3 :]
    make_weights(plan, steer, (wa, wb), wide, groups)
    columns(rest, yb)
    first[...] = partial[...]
    outer(even, 0, odd, th, tl, first, xh, xl)
    columns(first, ya)
    copies = []
    for start, stop in parts_of(out.shape[2]):
        lanes = slice(start * TILE, stop * TILE)
        dense[:, lanes] = dot(wa[...], ya[:, lanes]) + dot(wb[...], yb[:, lanes])
        copies += send(0, dense, out, start, stop, sems)
    for raw, result in zip(raws, partials):
        inner(raw, th, tl, result, xh, xl)
    for copy in copies:
        copy.wait()


def spill_kernel(parity, own, after, th, tl, out, xh, xl):
    span = th.shape[0] - 1

    @pl.when(lax.rem(lax.axis_index("range"), 2) == parity)
    def _():
        for part in range(2):
            place(jnp.swapaxes(own[part, :, own.shape[2] - span :], 0, 1), xh, xl, part)
        out[...] = jnp.zeros_like(out)
        spill(th, tl, out, xh, xl)


def ready_kernel(odd, rest, yb):
    columns(rest, yb)


def other_kernel(shift, yb, even, odd, partial, wa, wb, held, out, first, ya, dense, sems):
    index = lax.axis_index("range")
    count = even.shape[0]
    spilled = jnp.where(lax.rem(index, 2) == 1, even[...], odd[:count, :])
    spilled = jnp.where(index == 0, 0.0, spilled)
    first[...] = partial[...]
    first[:count, :] += spilled
    columns(first, ya)
    copies = []
    for start, stop in parts_of(out.shape[2]):
        lanes = slice(start * TILE, stop * TILE)
        dense[:, lanes] = dot(wa[...], ya[:, lanes]) + dot(wb[...], yb[:, lanes])
        copies += send(shift, dense, out, start, stop, sems)
    for copy in copies:
        copy.wait()


def call(kernel, name, out_shape, in_specs, out_specs, scratch_shapes, flops=1000, **kwargs):
    return pl.pallas_call(
        kernel,
        out_shape=out_shape,
        in_specs=in_specs,
        out_specs=out_specs,
        scratch_shapes=scratch_shapes,
        name=name,
        compiler_params=pltpu.CompilerParams(vmem_limit_bytes=16 << 20),
        cost_estimate=pl.CostEstimate(flops=flops, bytes_accessed=1000, transcendentals=0),
        **kwargs,
    )


def body(echoes, steer_blocks, plan, filter_taps):
    pulses = lax.axis_size("pulse")
    others = pulses - 1
    subarrays, gates = echoes.shape[1], echoes.shape[3]
    blocks = gates // TILE
    span = filter_taps.shape[1] // TILE
    assert echoes.shape[2] == 1 and blocks >= span and lax.axis_size("range") % 4 == 0
    cut = subarrays // 2
    left = subarrays - cut
    groups = ((0, cut), (cut, left))
    count = steer_blocks.shape[0] // plan.shape[1] * steer_blocks.shape[2]
    any_space = pl.BlockSpec(memory_space=pl.ANY)

    def shape(*dims, dtype=f32):
        return jax.ShapeDtypeStruct(dims, dtype)

    def halves(rows):
        return [pltpu.VMEM((blocks * rows, 2 * TILE), bf16)] * 2

    out_shape = shape(2, count, blocks, pulses, TILE)
    ya, yb = (pltpu.VMEM((6 * rows, gates), bf16) for rows in (cut, left))
    first = pltpu.VMEM((blocks * cut, 2 * TILE), f32)
    dense = [pltpu.VMEM((2 * count, gates), f32), pltpu.SemaphoreType.DMA((2 * blocks,))]

    samples = echoes.reshape(2, subarrays, blocks, TILE)
    tail = slice(blocks - span, blocks)
    raw, rest = samples[:, :cut], samples[:, cut:]
    odd_rest = from_odd(rest[:, :, tail])
    others_raw = [shifted(raw, "pulse", k) for k in range(1, pulses)]
    even = from_even(samples[:, :, tail])
    odd_raw = from_odd(raw[:, :, tail])

    th, tl, raw_partial, rest_partial = call(
        prepare_kernel,
        "prepare",
        [shape(span + 1, 2 * TILE, 2 * TILE, dtype=bf16)] * 2
        + [shape(blocks * rows, 2 * TILE) for rows in (cut, left)],
        [VMEM] * 3,
        [VMEM] * 4,
        [*halves(left), *halves(cut)],
    )(filter_taps, raw, rest)
    own_rest = call(
        functools.partial(rest_kernel, cut),
        "rest",
        shape(blocks * left + 8, 2 * TILE),
        [VMEM] * 5,
        VMEM,
        halves(left),
    )(even, odd_rest, rest_partial, th, tl)
    others_rest = [shifted(own_rest, "pulse", k) for k in range(1, pulses)]
    others_raw, own_rest = lax.optimization_barrier((others_raw, own_rest))
    def spilled(parity, raw, flops, more):
        return call(
            functools.partial(spill_kernel, parity),
            "spill",
            shape(span * cut + more, 2 * TILE),
            [VMEM, any_space, VMEM, VMEM],
            VMEM,
            [pltpu.VMEM((span * cut, 2 * TILE), bf16)] * 2,
            flops=flops,
        )(raw, own_rest, th, tl)

    odd_others = [from_odd(spilled(1, raw, 1 << 36, 0)) for raw in others_raw]
    even_others = [from_even(spilled(0, raw, 1000, 0)) for raw in others_raw]
    out, wa, wb, *partials = call(
        functools.partial(own_kernel, groups, others),
        "own",
        [out_shape]
        + [shape(2 * count, 6 * rows, dtype=bf16) for rows in (cut, left)]
        + [shape(blocks * cut, 2 * TILE)] * others,
        [VMEM] * (8 + others),
        [any_space] + [VMEM] * (2 + others),
        [first, *halves(cut), ya, yb, *dense, pltpu.VMEM((2 * subarrays, 2 * count), f32)],
    )(
        plan.T,
        steer_blocks.transpose(0, 1, 3, 2),
        even,
        odd_raw,
        raw_partial,
        own_rest,
        th,
        tl,
        *others_raw,
    )
    for k in range(1, pulses):
        ready = call(
            ready_kernel,
            "ready",
            shape(6 * left, gates, dtype=bf16),
            [any_space, VMEM],
            VMEM,
            [],
            flops=1 << 36,
        )(odd_others[k - 1], others_rest[k - 1])
        out = call(
            functools.partial(other_kernel, k),
            "other",
            out_shape,
            [VMEM] * 6 + [any_space],
            any_space,
            [first, ya, *dense],
            input_output_aliases={6: 0},
        )(ready, even_others[k - 1], odd_others[k - 1], partials[k - 1], wa, wb, out)
    return out.transpose(0, 1, 3, 2, 4).reshape(2, count, pulses, gates)


def solution(mesh):
    in_specs = (P(None, None, "pulse", "range"), P("pulse", None, None, None), P(), P())
    out_specs = P(None, "pulse", None, "range")
    return jax.shard_map(body, mesh=mesh, in_specs=in_specs, out_specs=out_specs, check_vma=False)
```

```python
import functools

import jax
import jax.numpy as jnp
from jax import lax
from jax.experimental import pallas as pl
from jax.experimental.pallas import tpu as pltpu
from jax.sharding import PartitionSpec as P

TILE = 128
f32 = jnp.float32
bf16 = jnp.bfloat16
VMEM = pl.BlockSpec(memory_space=pltpu.VMEM)
SMEM = pl.BlockSpec(memory_space=pltpu.SMEM)


def dot(left, right):
    return jnp.dot(left, right, preferred_element_type=f32)


def split(value):
    high = value.astype(bf16)
    return high, (value - high.astype(f32)).astype(bf16)


def shifted(value, axis, steps):
    count = lax.axis_size(axis)
    return lax.ppermute(value, axis, [(i, (i + steps) % count) for i in range(count)])


def from_odd(value):
    count = lax.axis_size("range")
    target = {i: (i + 1) % count for i in range(count)}
    source, goal = count - 1, count - 5
    while goal > 0:
        target[source] = goal
        source, goal = goal - 1, goal - 4
    target[source] = 0
    return lax.ppermute(value, "range", list(target.items()))


def from_even(value):
    count = lax.axis_size("range")
    return lax.ppermute(value, "range", [(i, i ^ 1) for i in range(count)])


def make_tables(taps_ref, high_ref, low_ref):
    span = taps_ref.shape[1] // TILE
    row = lax.broadcasted_iota(jnp.int32, (TILE, TILE), 0)
    lane = lax.broadcasted_iota(jnp.int32, (TILE, TILE), 1)
    upper = lane >= row
    before = [jnp.zeros((TILE, TILE), f32)] * 2
    for offset in range(span + 1):
        for part in range(2):
            if offset < span:
                taps = taps_ref[part : part + 1, offset * TILE : (offset + 1) * TILE]
                rolled = pltpu.roll(
                    jnp.broadcast_to(taps, (TILE, TILE)), 0, 1, stride=1, stride_axis=0
                )
            else:
                rolled = jnp.zeros((TILE, TILE), f32)
            table = jnp.where(upper, rolled, before[part])
            before[part] = rolled
            high, low = split(table)
            for ref, value in ((high_ref, high), (low_ref, low)):
                if part == 0:
                    ref[offset, :TILE, :TILE] = value
                    ref[offset, TILE:, TILE:] = value
                else:
                    ref[offset, :TILE, TILE:] = value
                    ref[offset, TILE:, :TILE] = -value


def make_weights(plan_ref, steer_ref, outs, wide, groups):
    per_beam = plan_ref.shape[0]
    sub, width = steer_ref.shape[2:]
    beam_blocks = steer_ref.shape[0] // per_beam
    beams = beam_blocks * width
    first = lax.axis_index("pulse") * beam_blocks
    column = lax.broadcasted_iota(jnp.int32, plan_ref.shape, 1)
    for i in range(beam_blocks):
        mine = jnp.sum(jnp.where(column == first + i, plan_ref[...], 0), axis=1, keepdims=True)
        chosen = [mine[k : k + 1] for k in range(per_beam)]
        left = slice(i * width, (i + 1) * width)
        right = slice(beams + i * width, beams + (i + 1) * width)
        for at, size in groups:
            for start in range(at, at + size, sub):
                real = imag = jnp.zeros((sub, width), f32)
                for k in range(per_beam):
                    here = jnp.broadcast_to(chosen[k] == start // sub, (sub, width))
                    real = jnp.where(here, steer_ref[i * per_beam + k, 0], real)
                    imag = jnp.where(here, steer_ref[i * per_beam + k, 1], imag)
                re_row = at + start
                im_row = re_row + size
                wide[re_row : re_row + sub, left] = real
                wide[im_row : im_row + sub, left] = -imag
                wide[re_row : re_row + sub, right] = imag
                wide[im_row : im_row + sub, right] = real
    for ref, (at, size) in zip(outs, groups):
        high, low = split(wide[2 * at : 2 * (at + size), :].T)
        ref[...] = jnp.concatenate([high, high, low], axis=1)


def place(value, xh, xl, part):
    blocks, rows = value.shape[:2]
    for block in range(blocks):
        high, low = split(value[block])
        at = (slice(block * rows, (block + 1) * rows), slice(part * TILE, (part + 1) * TILE))
        xh[at] = high
        xl[at] = low


def product(xh, xl, at, high, low):
    return dot(xh[at, :], high) + dot(xl[at, :], high) + dot(xh[at, :], low)


def inner(own_ref, high_ref, low_ref, out_ref, xh, xl):
    rows, blocks = own_ref.shape[1:3]
    span = high_ref.shape[0] - 1
    for part in range(2):
        place(jnp.swapaxes(own_ref[part], 0, 1), xh, xl, part)
    at = slice(0, blocks * rows)
    out_ref[...] = product(xh, xl, at, high_ref[0], low_ref[0])
    for offset in range(1, min(span + 1, blocks)):
        at = slice(0, (blocks - offset) * rows)
        out_ref[offset * rows :, :] += product(xh, xl, at, high_ref[offset], low_ref[offset])


def spill(high_ref, low_ref, out_ref, xh, xl, given=None):
    span = high_ref.shape[0] - 1
    rows = xh.shape[0] // span
    whole = product(xh, xl, slice(0, span * rows), high_ref[span], low_ref[span])
    out_ref[: span * rows, :] = whole if given is None else whole + given[: span * rows, :]
    for offset in range(1, span):
        at = slice((span - offset) * rows, span * rows)
        out_ref[: offset * rows, :] += product(xh, xl, at, high_ref[offset], low_ref[offset])


def outer(even_ref, start, odd_ref, given, high_ref, low_ref, out_ref, xh, xl):
    rows = odd_ref.shape[1]
    index = lax.axis_index("range")

    @pl.when(index > 0)
    def _():
        for part in range(2):
            value = even_ref[part, start : start + rows]
            value = jnp.where(lax.rem(index, 2) == 1, value, odd_ref[part])
            place(jnp.swapaxes(value, 0, 1), xh, xl, part)
        spill(high_ref, low_ref, out_ref, xh, xl, given)

    @pl.when(index == 0)
    def _():
        out_ref[...] = given[...]


def columns(ref, y):
    blocks = y.shape[1] // TILE
    rows = y.shape[0] // 6
    for block in range(blocks):
        lanes = slice(block * TILE, (block + 1) * TILE)
        for part in range(2):
            high, low = split(ref[block * rows : (block + 1) * rows, part * TILE : (part + 1) * TILE])
            for copy, value in enumerate((high, low, high)):
                base = (2 * copy + part) * rows
                y[base : base + rows, lanes] = value


def send(shift, dense, out_ref, start, stop, sems):
    count = dense.shape[0] // 2
    pulses = out_ref.shape[3]
    pulse = lax.rem(lax.axis_index("pulse") + pulses - shift, pulses)
    copies = []
    for block in range(start, stop):
        for part in range(2):
            copy = pltpu.make_async_copy(
                dense.at[part * count : (part + 1) * count, block * TILE : (block + 1) * TILE],
                out_ref.at[part, :, block, pulse, :],
                sems.at[2 * block + part],
            )
            copy.start()
            copies.append(copy)
    return copies


def parts_of(blocks):
    half = -(-blocks // 2)
    return [(0, half), (half, blocks)] if half < blocks else [(0, blocks)]


def prepare_kernel(taps, rest, th, tl, rest_partial, *scratch):
    make_tables(taps, th, tl)
    inner(rest, th, tl, rest_partial, *scratch[:2])


def rest_kernel(cut, even, odd, partial, th, tl, out, xh, xl):
    outer(even, cut, odd, partial, th, tl, out, xh, xl)


def own_kernel(groups, others, plan, steer, even, odd, own, rest, th, tl, *refs):
    raws, (out, wa, wb), partials = refs[:others], refs[others : others + 3], refs[others + 3 : 2 * others + 3]
    whole, first, xh, xl, ya, yb, dense, sems, wide = refs[2 * others + 3 :]
    make_weights(plan, steer, (wa, wb), wide, groups)
    columns(rest, yb)
    inner(own, th, tl, whole, xh, xl)
    outer(even, 0, odd, whole, th, tl, first, xh, xl)
    columns(first, ya)
    copies = []
    for start, stop in parts_of(out.shape[2]):
        lanes = slice(start * TILE, stop * TILE)
        dense[:, lanes] = dot(wa[...], ya[:, lanes]) + dot(wb[...], yb[:, lanes])
        copies += send(0, dense, out, start, stop, sems)
    for raw, result in zip(raws, partials):
        inner(raw, th, tl, result, xh, xl)
    for copy in copies:
        copy.wait()


def spill_kernel(parity, own, after, th, tl, out, xh, xl):
    span = th.shape[0] - 1

    @pl.when(lax.rem(lax.axis_index("range"), 2) == parity)
    def _():
        for part in range(2):
            place(jnp.swapaxes(own[part, :, own.shape[2] - span :], 0, 1), xh, xl, part)
        spill(th, tl, out, xh, xl)


def ready_kernel(rest, yb):
    columns(rest, yb)


def meet_kernel(odd, yb, token):
    token[...] = jnp.zeros_like(token)


def other_kernel(shift, yb, even, odd, partial, wa, wb, token, held, out, first, ya, dense, sems):
    index = lax.axis_index("range")
    count = even.shape[0]
    spilled = jnp.where(lax.rem(index, 2) == 1, even[...], odd[:count, :])
    spilled = jnp.where(index == 0, 0.0, spilled)
    first[...] = partial[...]
    first[:count, :] += spilled
    columns(first, ya)
    copies = []
    for start, stop in [(0, out.shape[2])]:
        lanes = slice(start * TILE, stop * TILE)
        dense[:, lanes] = dot(wa[...], ya[:, lanes]) + dot(wb[...], yb[:, lanes])
        copies += send(shift, dense, out, start, stop, sems)
    for copy in copies:
        copy.wait()


def call(kernel, name, out_shape, in_specs, out_specs, scratch_shapes, flops=1000, **kwargs):
    return pl.pallas_call(
        kernel,
        out_shape=out_shape,
        in_specs=in_specs,
        out_specs=out_specs,
        scratch_shapes=scratch_shapes,
        name=name,
        compiler_params=pltpu.CompilerParams(vmem_limit_bytes=16 << 20),
        cost_estimate=pl.CostEstimate(flops=flops, bytes_accessed=1000, transcendentals=0),
        **kwargs,
    )


def body(echoes, steer_blocks, plan, filter_taps):
    pulses = lax.axis_size("pulse")
    others = pulses - 1
    subarrays, gates = echoes.shape[1], echoes.shape[3]
    blocks = gates // TILE
    span = filter_taps.shape[1] // TILE
    assert echoes.shape[2] == 1 and blocks == span and lax.axis_size("range") % 4 == 0
    cut = subarrays // 2
    left = subarrays - cut
    groups = ((0, cut), (cut, left))
    count = steer_blocks.shape[0] // plan.shape[1] * steer_blocks.shape[2]
    any_space = pl.BlockSpec(memory_space=pl.ANY)

    def shape(*dims, dtype=f32):
        return jax.ShapeDtypeStruct(dims, dtype)

    def halves(rows):
        return [pltpu.VMEM((blocks * rows, 2 * TILE), bf16)] * 2

    out_shape = shape(2, count, blocks, pulses, TILE)
    ya, yb = (pltpu.VMEM((6 * rows, gates), bf16) for rows in (cut, left))
    first = pltpu.VMEM((blocks * cut, 2 * TILE), f32)
    dense = [pltpu.VMEM((2 * count, gates), f32), pltpu.SemaphoreType.DMA((2 * blocks,))]

    samples = echoes.reshape(2, subarrays, blocks, TILE)
    tail = slice(blocks - span, blocks)
    raw, rest = samples[:, :cut], samples[:, cut:]
    odd_rest = from_odd(rest[:, :, tail])
    others_raw = [shifted(raw, "pulse", k) for k in range(1, pulses)]
    even = from_even(samples[:, :, tail])
    odd_raw = from_odd(raw[:, :, tail])

    th, tl, rest_partial = call(
        prepare_kernel,
        "prepare",
        [shape(span + 1, 2 * TILE, 2 * TILE, dtype=bf16)] * 2
        + [shape(blocks * left, 2 * TILE)],
        [VMEM] * 2,
        [VMEM] * 3,
        halves(left),
    )(filter_taps, rest)
    own_rest = call(
        functools.partial(rest_kernel, cut),
        "rest",
        shape(blocks * left, 2 * TILE),
        [VMEM] * 5,
        VMEM,
        halves(left),
    )(even, odd_rest, rest_partial, th, tl)
    others_rest = [shifted(own_rest, "pulse", k) for k in range(1, pulses)]
    others_raw, own_rest = lax.optimization_barrier((others_raw, own_rest))
    def spilled(parity, raw, flops, more):
        return call(
            functools.partial(spill_kernel, parity),
            "spill",
            shape(span * cut + more, 2 * TILE),
            [VMEM, any_space, VMEM, VMEM],
            VMEM,
            [pltpu.VMEM((span * cut, 2 * TILE), bf16)] * 2,
            flops=flops,
        )(raw, own_rest, th, tl)

    odd_others = [from_odd(spilled(1, raw, 1 << 36, 0)) for raw in others_raw]
    even_others = [from_even(spilled(0, raw, 1000, 0)) for raw in others_raw]
    out, wa, wb, *partials = call(
        functools.partial(own_kernel, groups, others),
        "own",
        [out_shape]
        + [shape(2 * count, 6 * rows, dtype=bf16) for rows in (cut, left)]
        + [shape(blocks * cut, 2 * TILE)] * others,
        [VMEM] * (8 + others),
        [any_space] + [VMEM] * (2 + others),
        [first, first, *halves(cut), ya, yb, *dense, pltpu.VMEM((2 * subarrays, 2 * count), f32)],
    )(
        plan.T,
        steer_blocks.transpose(0, 1, 3, 2),
        even,
        odd_raw,
        raw,
        own_rest,
        th,
        tl,
        *others_raw,
    )
    for k in range(1, pulses):
        ready = call(
            ready_kernel,
            "ready",
            shape(6 * left, gates, dtype=bf16),
            [VMEM],
            VMEM,
            [],
            flops=1 << 30,
        )(others_rest[k - 1])
        token = call(
            meet_kernel, "meet", shape(8, TILE), [any_space] * 2, VMEM, [], flops=1 << 36
        )(odd_others[k - 1], ready)
        out = call(
            functools.partial(other_kernel, k),
            "other",
            out_shape,
            [VMEM] * 6 + [any_space] * 2,
            any_space,
            [first, ya, *dense],
            input_output_aliases={7: 0},
        )(ready, even_others[k - 1], odd_others[k - 1], partials[k - 1], wa, wb, token, out)
    return out.transpose(0, 1, 3, 2, 4).reshape(2, count, pulses, gates)


def solution(mesh):
    in_specs = (P(None, None, "pulse", "range"), P("pulse", None, None, None), P(), P())
    out_specs = P(None, "pulse", None, "range")
    return jax.shard_map(body, mesh=mesh, in_specs=in_specs, out_specs=out_specs, check_vma=False)
```

```python
import functools

import jax
import jax.numpy as jnp
from jax import lax
from jax.experimental import pallas as pl
from jax.experimental.pallas import tpu as pltpu
from jax.sharding import PartitionSpec as P

TILE = 128
f32 = jnp.float32
bf16 = jnp.bfloat16
VMEM = pl.BlockSpec(memory_space=pltpu.VMEM)
SMEM = pl.BlockSpec(memory_space=pltpu.SMEM)


def dot(left, right):
    return jnp.dot(left, right, preferred_element_type=f32)


def split(value):
    high = value.astype(bf16)
    return high, (value - high.astype(f32)).astype(bf16)


def shifted(value, axis, steps):
    count = lax.axis_size(axis)
    return lax.ppermute(value, axis, [(i, (i + steps) % count) for i in range(count)])


def from_odd(value):
    count = lax.axis_size("range")
    target = {i: (i + 1) % count for i in range(count)}
    source, goal = count - 1, count - 5
    while goal > 0:
        target[source] = goal
        source, goal = goal - 1, goal - 4
    target[source] = 0
    return lax.ppermute(value, "range", list(target.items()))


def from_even(value):
    count = lax.axis_size("range")
    return lax.ppermute(value, "range", [(i, i ^ 1) for i in range(count)])


def make_tables(taps_ref, high_ref, low_ref):
    span = taps_ref.shape[1] // TILE
    row = lax.broadcasted_iota(jnp.int32, (TILE, TILE), 0)
    lane = lax.broadcasted_iota(jnp.int32, (TILE, TILE), 1)
    upper = lane >= row
    before = [jnp.zeros((TILE, TILE), f32)] * 2
    for offset in range(span + 1):
        for part in range(2):
            if offset < span:
                taps = taps_ref[part : part + 1, offset * TILE : (offset + 1) * TILE]
                rolled = pltpu.roll(
                    jnp.broadcast_to(taps, (TILE, TILE)), 0, 1, stride=1, stride_axis=0
                )
            else:
                rolled = jnp.zeros((TILE, TILE), f32)
            table = jnp.where(upper, rolled, before[part])
            before[part] = rolled
            high, low = split(table)
            for ref, value in ((high_ref, high), (low_ref, low)):
                if part == 0:
                    ref[offset, :TILE, :TILE] = value
                    ref[offset, TILE:, TILE:] = value
                else:
                    ref[offset, :TILE, TILE:] = value
                    ref[offset, TILE:, :TILE] = -value


def make_weights(plan_ref, steer_ref, outs, wide, groups):
    per_beam = plan_ref.shape[0]
    sub, width = steer_ref.shape[2:]
    beam_blocks = steer_ref.shape[0] // per_beam
    beams = beam_blocks * width
    first = lax.axis_index("pulse") * beam_blocks
    column = lax.broadcasted_iota(jnp.int32, plan_ref.shape, 1)
    for i in range(beam_blocks):
        mine = jnp.sum(jnp.where(column == first + i, plan_ref[...], 0), axis=1, keepdims=True)
        chosen = [mine[k : k + 1] for k in range(per_beam)]
        left = slice(i * width, (i + 1) * width)
        right = slice(beams + i * width, beams + (i + 1) * width)
        for at, size in groups:
            for start in range(at, at + size, sub):
                real = imag = jnp.zeros((sub, width), f32)
                for k in range(per_beam):
                    here = jnp.broadcast_to(chosen[k] == start // sub, (sub, width))
                    real = jnp.where(here, steer_ref[i * per_beam + k, 0], real)
                    imag = jnp.where(here, steer_ref[i * per_beam + k, 1], imag)
                re_row = at + start
                im_row = re_row + size
                wide[re_row : re_row + sub, left] = real
                wide[im_row : im_row + sub, left] = -imag
                wide[re_row : re_row + sub, right] = imag
                wide[im_row : im_row + sub, right] = real
    for ref, (at, size) in zip(outs, groups):
        high, low = split(wide[2 * at : 2 * (at + size), :].T)
        ref[...] = jnp.concatenate([high, high, low], axis=1)


def place(value, block, xh, xl, part):
    rows = value.shape[0]
    high, low = split(value)
    at = (slice(block * rows, (block + 1) * rows), slice(part * TILE, (part + 1) * TILE))
    xh[at] = high
    xl[at] = low


def product(xh, xl, at, high, low):
    return dot(xh[at, :], high) + dot(xl[at, :], high) + dot(xh[at, :], low)


def inner(own_ref, high_ref, low_ref, out_ref, xh, xl):
    rows, blocks = own_ref.shape[1:3]
    span = high_ref.shape[0] - 1
    for part in range(2):
        value = jnp.swapaxes(own_ref[part], 0, 1)
        for block in range(blocks):
            place(value[block], block, xh, xl, part)
    at = slice(0, blocks * rows)
    out_ref[...] = product(xh, xl, at, high_ref[0], low_ref[0])
    for offset in range(1, min(span + 1, blocks)):
        at = slice(0, (blocks - offset) * rows)
        out_ref[offset * rows :, :] += product(xh, xl, at, high_ref[offset], low_ref[offset])


def spill(values, high_ref, low_ref, out_ref, xh, both, given=None):
    span = high_ref.shape[0] - 1
    rows = xh.shape[0] // span
    for offset in range(1, span + 1):
        block = span - offset
        for part in range(2):
            high, low = split(values[part][block])
            lanes = slice(part * TILE, (part + 1) * TILE)
            xh[block * rows : (block + 1) * rows, lanes] = high
            both[2 * block * rows : (2 * block + 1) * rows, lanes] = high
            both[(2 * block + 1) * rows : (2 * block + 2) * rows, lanes] = low
        pair = dot(both[2 * block * rows :, :], high_ref[offset])
        rest = dot(xh[block * rows :, :], low_ref[offset])
        for target in range(offset):
            at = slice(target * rows, (target + 1) * rows)
            term = pair[2 * target * rows : (2 * target + 1) * rows, :] + rest[at, :]
            term = term + pair[(2 * target + 1) * rows : (2 * target + 2) * rows, :]
            if target < offset - 1:
                out_ref[at, :] += term
            elif given is None:
                out_ref[at, :] = term
            else:
                out_ref[at, :] = term + given[at, :]


def outer(even_ref, start, odd_ref, given, high_ref, low_ref, out_ref, xh, xl):
    rows = odd_ref.shape[1]
    index = lax.axis_index("range")

    @pl.when(index > 0)
    def _():
        values = []
        for part in range(2):
            value = even_ref[part, start : start + rows]
            value = jnp.where(lax.rem(index, 2) == 1, value, odd_ref[part])
            values.append(jnp.swapaxes(value, 0, 1))
        spill(values, high_ref, low_ref, out_ref, xh, xl, given)

    @pl.when(index == 0)
    def _():
        out_ref[...] = given[...]


def columns(ref, y):
    blocks = y.shape[1] // TILE
    rows = y.shape[0] // 6
    for block in range(blocks):
        lanes = slice(block * TILE, (block + 1) * TILE)
        for part in range(2):
            high, low = split(ref[block * rows : (block + 1) * rows, part * TILE : (part + 1) * TILE])
            for copy, value in enumerate((high, low, high)):
                base = (2 * copy + part) * rows
                y[base : base + rows, lanes] = value


def send(shift, dense, out_ref, start, stop, sems):
    count = dense.shape[0] // 2
    pulses = out_ref.shape[3]
    pulse = lax.rem(lax.axis_index("pulse") + pulses - shift, pulses)
    copies = []
    for block in range(start, stop):
        for part in range(2):
            copy = pltpu.make_async_copy(
                dense.at[part * count : (part + 1) * count, block * TILE : (block + 1) * TILE],
                out_ref.at[part, :, block, pulse, :],
                sems.at[2 * block + part],
            )
            copy.start()
            copies.append(copy)
    return copies


def parts_of(blocks):
    half = -(-blocks // 2)
    return [(0, half), (half, blocks)] if half < blocks else [(0, blocks)]


def prepare_kernel(taps, rest, th, tl, rest_partial, *scratch):
    make_tables(taps, th, tl)
    inner(rest, th, tl, rest_partial, *scratch[:2])


def rest_kernel(cut, even, odd, partial, th, tl, out, xh, xl):
    outer(even, cut, odd, partial, th, tl, out, xh, xl)


def own_kernel(groups, others, plan, steer, even, odd, own, rest, th, tl, *refs):
    raws, (out, wa, wb), partials = refs[:others], refs[others : others + 3], refs[others + 3 : 2 * others + 3]
    whole, first, xh, xl, both, ya, yb, dense, sems, wide = refs[2 * others + 3 :]
    make_weights(plan, steer, (wa, wb), wide, groups)
    columns(rest, yb)
    inner(own, th, tl, whole, xh, xl)
    outer(even, 0, odd, whole, th, tl, first, xh, both)
    columns(first, ya)
    copies = []
    for start, stop in parts_of(out.shape[2]):
        lanes = slice(start * TILE, stop * TILE)
        dense[:, lanes] = dot(wa[...], ya[:, lanes]) + dot(wb[...], yb[:, lanes])
        copies += send(0, dense, out, start, stop, sems)
    for raw, result in zip(raws, partials):
        inner(raw, th, tl, result, xh, xl)
    for copy in copies:
        copy.wait()


def spill_kernel(parity, own, after, th, tl, out, xh, xl):
    span = th.shape[0] - 1

    @pl.when(lax.rem(lax.axis_index("range"), 2) == parity)
    def _():
        values = [jnp.swapaxes(own[part, :, own.shape[2] - span :], 0, 1) for part in range(2)]
        spill(values, th, tl, out, xh, xl)


def ready_kernel(rest, yb):
    columns(rest, yb)


def meet_kernel(odd, yb, token):
    token[...] = jnp.zeros_like(token)


def other_kernel(shift, yb, even, odd, partial, wa, wb, token, held, out, first, ya, dense, sems):
    index = lax.axis_index("range")
    count = even.shape[0]
    spilled = jnp.where(lax.rem(index, 2) == 1, even[...], odd[:count, :])
    spilled = jnp.where(index == 0, 0.0, spilled)
    first[...] = partial[...]
    first[:count, :] += spilled
    columns(first, ya)
    copies = []
    for start, stop in [(0, out.shape[2])]:
        lanes = slice(start * TILE, stop * TILE)
        dense[:, lanes] = dot(wa[...], ya[:, lanes]) + dot(wb[...], yb[:, lanes])
        copies += send(shift, dense, out, start, stop, sems)
    for copy in copies:
        copy.wait()


def call(kernel, name, out_shape, in_specs, out_specs, scratch_shapes, flops=1000, **kwargs):
    return pl.pallas_call(
        kernel,
        out_shape=out_shape,
        in_specs=in_specs,
        out_specs=out_specs,
        scratch_shapes=scratch_shapes,
        name=name,
        compiler_params=pltpu.CompilerParams(vmem_limit_bytes=16 << 20),
        cost_estimate=pl.CostEstimate(flops=flops, bytes_accessed=1000, transcendentals=0),
        **kwargs,
    )


def body(echoes, steer_blocks, plan, filter_taps):
    pulses = lax.axis_size("pulse")
    others = pulses - 1
    subarrays, gates = echoes.shape[1], echoes.shape[3]
    blocks = gates // TILE
    span = filter_taps.shape[1] // TILE
    assert echoes.shape[2] == 1 and blocks == span and lax.axis_size("range") % 4 == 0
    cut = subarrays // 2
    left = subarrays - cut
    groups = ((0, cut), (cut, left))
    count = steer_blocks.shape[0] // plan.shape[1] * steer_blocks.shape[2]
    any_space = pl.BlockSpec(memory_space=pl.ANY)

    def shape(*dims, dtype=f32):
        return jax.ShapeDtypeStruct(dims, dtype)

    def halves(rows):
        return [pltpu.VMEM((blocks * rows, 2 * TILE), bf16)] * 2

    def spilling(rows):
        return [pltpu.VMEM((k * span * rows, 2 * TILE), bf16) for k in (1, 2)]

    out_shape = shape(2, count, blocks, pulses, TILE)
    ya, yb = (pltpu.VMEM((6 * rows, gates), bf16) for rows in (cut, left))
    first = pltpu.VMEM((blocks * cut, 2 * TILE), f32)
    dense = [pltpu.VMEM((2 * count, gates), f32), pltpu.SemaphoreType.DMA((2 * blocks,))]

    samples = echoes.reshape(2, subarrays, blocks, TILE)
    tail = slice(blocks - span, blocks)
    raw, rest = samples[:, :cut], samples[:, cut:]
    odd_rest = from_odd(rest[:, :, tail])
    others_raw = [shifted(raw, "pulse", k) for k in range(1, pulses)]
    even = from_even(samples[:, :, tail])
    odd_raw = from_odd(raw[:, :, tail])

    th, tl, rest_partial = call(
        prepare_kernel,
        "prepare",
        [shape(span + 1, 2 * TILE, 2 * TILE, dtype=bf16)] * 2
        + [shape(blocks * left, 2 * TILE)],
        [VMEM] * 2,
        [VMEM] * 3,
        halves(left),
    )(filter_taps, rest)
    own_rest = call(
        functools.partial(rest_kernel, cut),
        "rest",
        shape(blocks * left, 2 * TILE),
        [VMEM] * 5,
        VMEM,
        spilling(left),
    )(even, odd_rest, rest_partial, th, tl)
    others_rest = [shifted(own_rest, "pulse", k) for k in range(1, pulses)]
    others_raw, own_rest = lax.optimization_barrier((others_raw, own_rest))
    def spilled(parity, raw, flops, more):
        return call(
            functools.partial(spill_kernel, parity),
            "spill",
            shape(span * cut + more, 2 * TILE),
            [VMEM, any_space, VMEM, VMEM],
            VMEM,
            spilling(cut),
            flops=flops,
        )(raw, own_rest, th, tl)

    odd_others = [from_odd(spilled(1, raw, 1 << 36, 0)) for raw in others_raw]
    even_others = [from_even(spilled(0, raw, 1000, 0)) for raw in others_raw]
    out, wa, wb, *partials = call(
        functools.partial(own_kernel, groups, others),
        "own",
        [out_shape]
        + [shape(2 * count, 6 * rows, dtype=bf16) for rows in (cut, left)]
        + [shape(blocks * cut, 2 * TILE)] * others,
        [VMEM] * (8 + others),
        [any_space] + [VMEM] * (2 + others),
        [first, first, *halves(cut), spilling(cut)[1], ya, yb, *dense, pltpu.VMEM((2 * subarrays, 2 * count), f32)],
    )(
        plan.T,
        steer_blocks.transpose(0, 1, 3, 2),
        even,
        odd_raw,
        raw,
        own_rest,
        th,
        tl,
        *others_raw,
    )
    for k in range(1, pulses):
        ready = call(
            ready_kernel,
            "ready",
            shape(6 * left, gates, dtype=bf16),
            [VMEM],
            VMEM,
            [],
            flops=1 << 30,
        )(others_rest[k - 1])
        token = call(
            meet_kernel, "meet", shape(8, TILE), [any_space] * 2, VMEM, [], flops=1 << 36
        )(odd_others[k - 1], ready)
        out = call(
            functools.partial(other_kernel, k),
            "other",
            out_shape,
            [VMEM] * 6 + [any_space] * 2,
            any_space,
            [first, ya, *dense],
            input_output_aliases={7: 0},
        )(ready, even_others[k - 1], odd_others[k - 1], partials[k - 1], wa, wb, token, out)
    return out.transpose(0, 1, 3, 2, 4).reshape(2, count, pulses, gates)


def solution(mesh):
    in_specs = (P(None, None, "pulse", "range"), P("pulse", None, None, None), P(), P())
    out_specs = P(None, "pulse", None, "range")
    return jax.shard_map(body, mesh=mesh, in_specs=in_specs, out_specs=out_specs, check_vma=False)
```

```python
import functools

import jax
import jax.numpy as jnp
from jax import lax
from jax.experimental import pallas as pl
from jax.experimental.pallas import tpu as pltpu
from jax.sharding import PartitionSpec as P

TILE = 128
f32 = jnp.float32
bf16 = jnp.bfloat16
VMEM = pl.BlockSpec(memory_space=pltpu.VMEM)
SMEM = pl.BlockSpec(memory_space=pltpu.SMEM)


def dot(left, right):
    return jnp.dot(left, right, preferred_element_type=f32)


def split(value):
    high = value.astype(bf16)
    return high, (value - high.astype(f32)).astype(bf16)


def shifted(value, axis, steps):
    count = lax.axis_size(axis)
    return lax.ppermute(value, axis, [(i, (i + steps) % count) for i in range(count)])


def from_odd(value):
    count = lax.axis_size("range")
    target = {i: (i + 1) % count for i in range(count)}
    source, goal = count - 1, count - 5
    while goal > 0:
        target[source] = goal
        source, goal = goal - 1, goal - 4
    target[source] = 0
    return lax.ppermute(value, "range", list(target.items()))


def from_even(value):
    count = lax.axis_size("range")
    return lax.ppermute(value, "range", [(i, i ^ 1) for i in range(count)])


def make_tables(taps_ref, high_ref, low_ref):
    span = taps_ref.shape[1] // TILE
    row = lax.broadcasted_iota(jnp.int32, (TILE, TILE), 0)
    lane = lax.broadcasted_iota(jnp.int32, (TILE, TILE), 1)
    upper = lane >= row
    before = [jnp.zeros((TILE, TILE), f32)] * 2
    for offset in range(span + 1):
        for part in range(2):
            if offset < span:
                taps = taps_ref[part : part + 1, offset * TILE : (offset + 1) * TILE]
                rolled = pltpu.roll(
                    jnp.broadcast_to(taps, (TILE, TILE)), 0, 1, stride=1, stride_axis=0
                )
            else:
                rolled = jnp.zeros((TILE, TILE), f32)
            table = jnp.where(upper, rolled, before[part])
            before[part] = rolled
            high, low = split(table)
            for ref, value in ((high_ref, high), (low_ref, low)):
                if part == 0:
                    ref[offset, :TILE, :TILE] = value
                    ref[offset, TILE:, TILE:] = value
                else:
                    ref[offset, :TILE, TILE:] = value
                    ref[offset, TILE:, :TILE] = -value


def make_weights(plan_ref, steer_ref, outs, wide, groups):
    per_beam = plan_ref.shape[0]
    sub, width = steer_ref.shape[2:]
    beam_blocks = steer_ref.shape[0] // per_beam
    beams = beam_blocks * width
    first = lax.axis_index("pulse") * beam_blocks
    column = lax.broadcasted_iota(jnp.int32, plan_ref.shape, 1)
    for i in range(beam_blocks):
        mine = jnp.sum(jnp.where(column == first + i, plan_ref[...], 0), axis=1, keepdims=True)
        chosen = [mine[k : k + 1] for k in range(per_beam)]
        left = slice(i * width, (i + 1) * width)
        right = slice(beams + i * width, beams + (i + 1) * width)
        for at, size in groups:
            for start in range(at, at + size, sub):
                real = imag = jnp.zeros((sub, width), f32)
                for k in range(per_beam):
                    here = jnp.broadcast_to(chosen[k] == start // sub, (sub, width))
                    real = jnp.where(here, steer_ref[i * per_beam + k, 0], real)
                    imag = jnp.where(here, steer_ref[i * per_beam + k, 1], imag)
                re_row = at + start
                im_row = re_row + size
                wide[re_row : re_row + sub, left] = real
                wide[im_row : im_row + sub, left] = -imag
                wide[re_row : re_row + sub, right] = imag
                wide[im_row : im_row + sub, right] = real
    for ref, (at, size) in zip(outs, groups):
        high, low = split(wide[2 * at : 2 * (at + size), :].T)
        ref[...] = jnp.concatenate([high, high, low], axis=1)


def place(value, block, xh, xl, part):
    rows = value.shape[0]
    high, low = split(value)
    at = (slice(block * rows, (block + 1) * rows), slice(part * TILE, (part + 1) * TILE))
    xh[at] = high
    xl[at] = low


def product(xh, xl, at, high, low):
    return dot(xh[at, :], high) + dot(xl[at, :], high) + dot(xh[at, :], low)


def inner(own_ref, high_ref, low_ref, out_ref, xh, xl):
    rows, blocks = own_ref.shape[1:3]
    span = high_ref.shape[0] - 1
    for part in range(2):
        value = jnp.swapaxes(own_ref[part], 0, 1)
        for block in range(blocks):
            place(value[block], block, xh, xl, part)
    at = slice(0, blocks * rows)
    out_ref[...] = product(xh, xl, at, high_ref[0], low_ref[0])
    for offset in range(1, min(span + 1, blocks)):
        at = slice(0, (blocks - offset) * rows)
        out_ref[offset * rows :, :] += product(xh, xl, at, high_ref[offset], low_ref[offset])


def spill(values, high_ref, low_ref, out_ref, xh, both, given=None):
    span = high_ref.shape[0] - 1
    rows = xh.shape[0] // span
    for offset in range(1, span + 1):
        block = span - offset
        for part in range(2):
            high, low = split(values[part][block])
            lanes = slice(part * TILE, (part + 1) * TILE)
            xh[block * rows : (block + 1) * rows, lanes] = high
            both[2 * block * rows : (2 * block + 1) * rows, lanes] = high
            both[(2 * block + 1) * rows : (2 * block + 2) * rows, lanes] = low
        pair = dot(both[2 * block * rows :, :], high_ref[offset])
        rest = dot(xh[block * rows :, :], low_ref[offset])
        for target in range(offset):
            at = slice(target * rows, (target + 1) * rows)
            term = pair[2 * target * rows : (2 * target + 1) * rows, :] + rest[at, :]
            term = term + pair[(2 * target + 1) * rows : (2 * target + 2) * rows, :]
            if target < offset - 1:
                out_ref[at, :] += term
            elif given is None:
                out_ref[at, :] = term
            else:
                out_ref[at, :] = term + given[at, :]


def outer(even_ref, start, odd_ref, given, high_ref, low_ref, out_ref, xh, xl):
    rows = odd_ref.shape[1]
    index = lax.axis_index("range")

    @pl.when(index > 0)
    def _():
        values = []
        for part in range(2):
            value = even_ref[part, start : start + rows]
            value = jnp.where(lax.rem(index, 2) == 1, value, odd_ref[part])
            values.append(jnp.swapaxes(value, 0, 1))
        spill(values, high_ref, low_ref, out_ref, xh, xl, given)

    @pl.when(index == 0)
    def _():
        out_ref[...] = given[...]


def columns(ref, y):
    blocks = y.shape[1] // TILE
    rows = y.shape[0] // 6
    for block in range(blocks):
        lanes = slice(block * TILE, (block + 1) * TILE)
        for part in range(2):
            high, low = split(ref[block * rows : (block + 1) * rows, part * TILE : (part + 1) * TILE])
            for copy, value in enumerate((high, low, high)):
                base = (2 * copy + part) * rows
                y[base : base + rows, lanes] = value


def send(shift, dense, out_ref, start, stop, sems):
    pulses = out_ref.shape[2]
    pulse = lax.rem(lax.axis_index("pulse") + pulses - shift, pulses)
    copies = []
    for block in range(start, stop):
        copy = pltpu.make_async_copy(
            dense.at[:, block * TILE : (block + 1) * TILE],
            out_ref.at[:, block, pulse, :],
            sems.at[block],
        )
        copy.start()
        copies.append(copy)
    return copies


def parts_of(blocks):
    half = -(-blocks // 2)
    return [(0, half), (half, blocks)] if half < blocks else [(0, blocks)]


def prepare_kernel(taps, rest, th, tl, rest_partial, *scratch):
    make_tables(taps, th, tl)
    inner(rest, th, tl, rest_partial, *scratch[:2])


def rest_kernel(cut, even, odd, partial, th, tl, out, xh, xl):
    outer(even, cut, odd, partial, th, tl, out, xh, xl)


def own_kernel(groups, others, plan, steer, even, odd, own, rest, th, tl, *refs):
    raws, (out, wa, wb), partials = refs[:others], refs[others : others + 3], refs[others + 3 : 2 * others + 3]
    whole, first, xh, xl, both, ya, yb, dense, sems, wide = refs[2 * others + 3 :]
    make_weights(plan, steer, (wa, wb), wide, groups)
    columns(rest, yb)
    inner(own, th, tl, whole, xh, xl)
    outer(even, 0, odd, whole, th, tl, first, xh, both)
    columns(first, ya)
    copies = []
    for start, stop in parts_of(out.shape[1]):
        lanes = slice(start * TILE, stop * TILE)
        dense[:, lanes] = dot(wa[...], ya[:, lanes]) + dot(wb[...], yb[:, lanes])
        copies += send(0, dense, out, start, stop, sems)
    for raw, result in zip(raws, partials):
        inner(raw, th, tl, result, xh, xl)
    for copy in copies:
        copy.wait()


def spill_kernel(parity, own, after, th, tl, out, xh, xl):
    span = th.shape[0] - 1

    @pl.when(lax.rem(lax.axis_index("range"), 2) == parity)
    def _():
        values = [jnp.swapaxes(own[part, :, own.shape[2] - span :], 0, 1) for part in range(2)]
        spill(values, th, tl, out, xh, xl)


def ready_kernel(rest, yb):
    columns(rest, yb)


def meet_kernel(odd, yb, token):
    token[...] = jnp.zeros_like(token)


def other_kernel(shift, yb, even, odd, partial, wa, wb, token, held, out, first, ya, dense, sems):
    index = lax.axis_index("range")
    count = even.shape[0]
    spilled = jnp.where(lax.rem(index, 2) == 1, even[...], odd[:count, :])
    spilled = jnp.where(index == 0, 0.0, spilled)
    first[...] = partial[...]
    first[:count, :] += spilled
    columns(first, ya)
    copies = []
    for start, stop in [(0, out.shape[1])]:
        lanes = slice(start * TILE, stop * TILE)
        dense[:, lanes] = dot(wa[...], ya[:, lanes]) + dot(wb[...], yb[:, lanes])
        copies += send(shift, dense, out, start, stop, sems)
    for copy in copies:
        copy.wait()


def call(kernel, name, out_shape, in_specs, out_specs, scratch_shapes, flops=1000, **kwargs):
    return pl.pallas_call(
        kernel,
        out_shape=out_shape,
        in_specs=in_specs,
        out_specs=out_specs,
        scratch_shapes=scratch_shapes,
        name=name,
        compiler_params=pltpu.CompilerParams(vmem_limit_bytes=16 << 20),
        cost_estimate=pl.CostEstimate(flops=flops, bytes_accessed=1000, transcendentals=0),
        **kwargs,
    )


def body(echoes, steer_blocks, plan, filter_taps):
    pulses = lax.axis_size("pulse")
    others = pulses - 1
    subarrays, gates = echoes.shape[1], echoes.shape[3]
    blocks = gates // TILE
    span = filter_taps.shape[1] // TILE
    assert echoes.shape[2] == 1 and blocks == span and lax.axis_size("range") % 4 == 0
    cut = subarrays // 2
    left = subarrays - cut
    groups = ((0, cut), (cut, left))
    count = steer_blocks.shape[0] // plan.shape[1] * steer_blocks.shape[2]
    any_space = pl.BlockSpec(memory_space=pl.ANY)

    def shape(*dims, dtype=f32):
        return jax.ShapeDtypeStruct(dims, dtype)

    def halves(rows):
        return [pltpu.VMEM((blocks * rows, 2 * TILE), bf16)] * 2

    def spilling(rows):
        return [pltpu.VMEM((k * span * rows, 2 * TILE), bf16) for k in (1, 2)]

    out_shape = shape(2 * count, blocks, pulses, TILE)
    ya, yb = (pltpu.VMEM((6 * rows, gates), bf16) for rows in (cut, left))
    first = pltpu.VMEM((blocks * cut, 2 * TILE), f32)
    dense = [pltpu.VMEM((2 * count, gates), f32), pltpu.SemaphoreType.DMA((blocks,))]

    samples = echoes.reshape(2, subarrays, blocks, TILE)
    tail = slice(blocks - span, blocks)
    raw, rest = samples[:, :cut], samples[:, cut:]
    odd_rest = from_odd(rest[:, :, tail])
    others_raw = [shifted(raw, "pulse", k) for k in range(1, pulses)]
    even = from_even(samples[:, :, tail])
    odd_raw = from_odd(raw[:, :, tail])

    th, tl, rest_partial = call(
        prepare_kernel,
        "prepare",
        [shape(span + 1, 2 * TILE, 2 * TILE, dtype=bf16)] * 2
        + [shape(blocks * left, 2 * TILE)],
        [VMEM] * 2,
        [VMEM] * 3,
        halves(left),
    )(filter_taps, rest)
    own_rest = call(
        functools.partial(rest_kernel, cut),
        "rest",
        shape(blocks * left, 2 * TILE),
        [VMEM] * 5,
        VMEM,
        spilling(left),
    )(even, odd_rest, rest_partial, th, tl)
    others_rest = [shifted(own_rest, "pulse", k) for k in range(1, pulses)]
    others_raw, own_rest = lax.optimization_barrier((others_raw, own_rest))
    def spilled(parity, raw, flops, more):
        return call(
            functools.partial(spill_kernel, parity),
            "spill",
            shape(span * cut + more, 2 * TILE),
            [VMEM, any_space, VMEM, VMEM],
            VMEM,
            spilling(cut),
            flops=flops,
        )(raw, own_rest, th, tl)

    odd_others = [from_odd(spilled(1, raw, 1 << 36, 0)) for raw in others_raw]
    even_others = [from_even(spilled(0, raw, 1000, 0)) for raw in others_raw]
    out, wa, wb, *partials = call(
        functools.partial(own_kernel, groups, others),
        "own",
        [out_shape]
        + [shape(2 * count, 6 * rows, dtype=bf16) for rows in (cut, left)]
        + [shape(blocks * cut, 2 * TILE)] * others,
        [VMEM] * (8 + others),
        [any_space] + [VMEM] * (2 + others),
        [first, first, *halves(cut), spilling(cut)[1], ya, yb, *dense, pltpu.VMEM((2 * subarrays, 2 * count), f32)],
    )(
        plan.T,
        steer_blocks.transpose(0, 1, 3, 2),
        even,
        odd_raw,
        raw,
        own_rest,
        th,
        tl,
        *others_raw,
    )
    for k in range(1, pulses):
        ready = call(
            ready_kernel,
            "ready",
            shape(6 * left, gates, dtype=bf16),
            [VMEM],
            VMEM,
            [],
            flops=1 << 30,
        )(others_rest[k - 1])
        token = call(
            meet_kernel, "meet", shape(8, TILE), [any_space] * 2, VMEM, [], flops=1 << 36
        )(odd_others[k - 1], ready)
        out = call(
            functools.partial(other_kernel, k),
            "other",
            out_shape,
            [VMEM] * 6 + [any_space] * 2,
            any_space,
            [first, ya, *dense],
            input_output_aliases={7: 0},
        )(ready, even_others[k - 1], odd_others[k - 1], partials[k - 1], wa, wb, token, out)
    return out.transpose(0, 2, 1, 3).reshape(2, count, pulses, gates)


def solution(mesh):
    in_specs = (P(None, None, "pulse", "range"), P("pulse", None, None, None), P(), P())
    out_specs = P(None, "pulse", None, "range")
    return jax.shard_map(body, mesh=mesh, in_specs=in_specs, out_specs=out_specs, check_vma=False)
```

```python
import functools

import jax
import jax.numpy as jnp
from jax import lax
from jax.experimental import pallas as pl
from jax.experimental.pallas import tpu as pltpu
from jax.sharding import PartitionSpec as P

TILE = 128
f32 = jnp.float32
bf16 = jnp.bfloat16
VMEM = pl.BlockSpec(memory_space=pltpu.VMEM)
SHORT, LONG = 1000, 1 << 36


def dot(left, right):
    return jnp.dot(left, right, preferred_element_type=f32)


def split(value):
    high = value.astype(bf16)
    return high, (value - high.astype(f32)).astype(bf16)


def shifted(value, axis, steps):
    count = lax.axis_size(axis)
    return lax.ppermute(value, axis, [(i, (i + steps) % count) for i in range(count)])


def from_odd(value):
    count = lax.axis_size("range")
    target = {i: (i + 1) % count for i in range(count)}
    source, goal = count - 1, count - 5
    while goal > 0:
        target[source] = goal
        source, goal = goal - 1, goal - 4
    target[source] = 0
    return lax.ppermute(value, "range", list(target.items()))


def from_even(value):
    count = lax.axis_size("range")
    return lax.ppermute(value, "range", [(i, i ^ 1) for i in range(count)])


def make_tables(taps_ref, high_ref, low_ref):
    span = taps_ref.shape[1] // TILE
    row = lax.broadcasted_iota(jnp.int32, (TILE, TILE), 0)
    lane = lax.broadcasted_iota(jnp.int32, (TILE, TILE), 1)
    upper = lane >= row
    before = [jnp.zeros((TILE, TILE), f32)] * 2
    for offset in range(span + 1):
        for part in range(2):
            if offset < span:
                taps = taps_ref[part : part + 1, offset * TILE : (offset + 1) * TILE]
                rolled = pltpu.roll(
                    jnp.broadcast_to(taps, (TILE, TILE)), 0, 1, stride=1, stride_axis=0
                )
            else:
                rolled = jnp.zeros((TILE, TILE), f32)
            table = jnp.where(upper, rolled, before[part])
            before[part] = rolled
            high, low = split(table)
            for ref, value in ((high_ref, high), (low_ref, low)):
                if part == 0:
                    ref[offset, :TILE, :TILE] = value
                    ref[offset, TILE:, TILE:] = value
                else:
                    ref[offset, :TILE, TILE:] = value
                    ref[offset, TILE:, :TILE] = -value


def make_weights(plan_ref, steer_ref, outs, wide, groups):
    per_beam = plan_ref.shape[0]
    sub, width = steer_ref.shape[2:]
    beam_blocks = steer_ref.shape[0] // per_beam
    beams = beam_blocks * width
    first = lax.axis_index("pulse") * beam_blocks
    column = lax.broadcasted_iota(jnp.int32, plan_ref.shape, 1)
    for i in range(beam_blocks):
        mine = jnp.sum(jnp.where(column == first + i, plan_ref[...], 0), axis=1, keepdims=True)
        chosen = [mine[k : k + 1] for k in range(per_beam)]
        left = slice(i * width, (i + 1) * width)
        right = slice(beams + i * width, beams + (i + 1) * width)
        for at, size in groups:
            for start in range(at, at + size, sub):
                real = imag = jnp.zeros((sub, width), f32)
                for k in range(per_beam):
                    here = jnp.broadcast_to(chosen[k] == start // sub, (sub, width))
                    real = jnp.where(here, steer_ref[i * per_beam + k, 0], real)
                    imag = jnp.where(here, steer_ref[i * per_beam + k, 1], imag)
                re_row = at + start
                im_row = re_row + size
                wide[re_row : re_row + sub, left] = real
                wide[im_row : im_row + sub, left] = -imag
                wide[re_row : re_row + sub, right] = imag
                wide[im_row : im_row + sub, right] = real
    for ref, (at, size) in zip(outs, groups):
        high, low = split(wide[2 * at : 2 * (at + size), :].T)
        ref[...] = jnp.concatenate([high, high, low], axis=1)


def place(value, block, xh, xl, part):
    rows = value.shape[0]
    high, low = split(value)
    at = (slice(block * rows, (block + 1) * rows), slice(part * TILE, (part + 1) * TILE))
    xh[at] = high
    xl[at] = low


def product(xh, xl, at, high, low):
    return dot(xh[at, :], high) + dot(xl[at, :], high) + dot(xh[at, :], low)


def inner(own_ref, high_ref, low_ref, out_ref, xh, xl):
    rows, blocks = own_ref.shape[1:3]
    span = high_ref.shape[0] - 1
    for part in range(2):
        value = jnp.swapaxes(own_ref[part], 0, 1)
        for block in range(blocks):
            place(value[block], block, xh, xl, part)
    at = slice(0, blocks * rows)
    out_ref[...] = product(xh, xl, at, high_ref[0], low_ref[0])
    for offset in range(1, min(span + 1, blocks)):
        at = slice(0, (blocks - offset) * rows)
        out_ref[offset * rows :, :] += product(xh, xl, at, high_ref[offset], low_ref[offset])


def spill(values, high_ref, low_ref, out_ref, xh, both, given=None):
    span = high_ref.shape[0] - 1
    rows = xh.shape[0] // span
    for offset in range(1, span + 1):
        block = span - offset
        for part in range(2):
            high, low = split(values[part][block])
            lanes = slice(part * TILE, (part + 1) * TILE)
            xh[block * rows : (block + 1) * rows, lanes] = high
            both[2 * block * rows : (2 * block + 1) * rows, lanes] = high
            both[(2 * block + 1) * rows : (2 * block + 2) * rows, lanes] = low
        pair = dot(both[2 * block * rows :, :], high_ref[offset])
        rest = dot(xh[block * rows :, :], low_ref[offset])
        for target in range(offset):
            at = slice(target * rows, (target + 1) * rows)
            term = pair[2 * target * rows : (2 * target + 1) * rows, :] + rest[at, :]
            term = term + pair[(2 * target + 1) * rows : (2 * target + 2) * rows, :]
            if target < offset - 1:
                out_ref[at, :] += term
            elif given is None:
                out_ref[at, :] = term
            else:
                out_ref[at, :] = term + given[at, :]


def outer(even_ref, start, odd_ref, given, high_ref, low_ref, out_ref, xh, xl):
    rows = odd_ref.shape[1]
    index = lax.axis_index("range")

    @pl.when(index > 0)
    def _():
        values = []
        for part in range(2):
            value = even_ref[part, start : start + rows]
            value = jnp.where(lax.rem(index, 2) == 1, value, odd_ref[part])
            values.append(jnp.swapaxes(value, 0, 1))
        spill(values, high_ref, low_ref, out_ref, xh, xl, given)

    @pl.when(index == 0)
    def _():
        out_ref[...] = given[...]


def columns(ref, y, added=None):
    blocks = y.shape[1] // TILE
    rows = y.shape[0] // 6
    for block in range(blocks):
        lanes = slice(block * TILE, (block + 1) * TILE)
        at = slice(block * rows, (block + 1) * rows)
        total = ref[at, :] if added is None else ref[at, :] + added[at, :]
        for part in range(2):
            high, low = split(total[:, part * TILE : (part + 1) * TILE])
            for copy, value in enumerate((high, low, high)):
                base = (2 * copy + part) * rows
                y[base : base + rows, lanes] = value


def send(shift, dense, out_ref, start, stop, sems):
    pulses = out_ref.shape[2]
    pulse = lax.rem(lax.axis_index("pulse") + pulses - shift, pulses)
    copies = []
    for block in range(start, stop):
        copy = pltpu.make_async_copy(
            dense.at[:, block * TILE : (block + 1) * TILE],
            out_ref.at[:, block, pulse, :],
            sems.at[block],
        )
        copy.start()
        copies.append(copy)
    return copies


def parts_of(blocks):
    half = -(-blocks // 2)
    return [(0, half), (half, blocks)] if half < blocks else [(0, blocks)]


def prepare_kernel(taps, rest, th, tl, partial, xh, xl):
    make_tables(taps, th, tl)
    inner(rest, th, tl, partial, xh, xl)


def rest_kernel(cut, even, odd, partial, th, tl, out, xh, xl):
    outer(even, cut, odd, partial, th, tl, out, xh, xl)


def own_kernel(groups, others, plan, steer, even, odd, own, rest, th, tl, *refs):
    raws, (out, wa, wb), partials = refs[:others], refs[others : others + 3], refs[others + 3 : 2 * others + 3]
    whole, first, xh, xl, both, ya, yb, dense, sems, wide = refs[2 * others + 3 :]
    make_weights(plan, steer, (wa, wb), wide, groups)
    columns(rest, yb)
    inner(own, th, tl, whole, xh, xl)
    outer(even, 0, odd, whole, th, tl, first, xh, both)
    columns(first, ya)
    copies = []
    for start, stop in parts_of(out.shape[1]):
        lanes = slice(start * TILE, stop * TILE)
        dense[:, lanes] = dot(wa[...], ya[:, lanes]) + dot(wb[...], yb[:, lanes])
        copies += send(0, dense, out, start, stop, sems)
    for raw, result in zip(raws, partials):
        inner(raw, th, tl, result, xh, xl)
    for copy in copies:
        copy.wait()


def spill_kernel(parity, own, after, th, tl, out, xh, xl):
    span = th.shape[0] - 1

    @pl.when(lax.rem(lax.axis_index("range"), 2) == parity)
    def _():
        values = [jnp.swapaxes(own[part, :, own.shape[2] - span :], 0, 1) for part in range(2)]
        spill(values, th, tl, out, xh, xl)


def ready_kernel(rest, yb):
    columns(rest, yb)


def meet_kernel(odd, yb, token):
    token[...] = jnp.zeros_like(token)


def other_kernel(shift, yb, even, odd, partial, wa, wb, token, held, out, ya, dense, sems):
    index = lax.axis_index("range")
    spilled = jnp.where(lax.rem(index, 2) == 1, even[...], odd[...])
    columns(partial, ya, jnp.where(index == 0, 0.0, spilled))
    dense[...] = dot(wa[...], ya[...]) + dot(wb[...], yb[...])
    for copy in send(shift, dense, out, 0, out.shape[1], sems):
        copy.wait()


def call(kernel, name, out_shape, in_specs, out_specs, scratch_shapes, flops=SHORT, **kwargs):
    return pl.pallas_call(
        kernel,
        out_shape=out_shape,
        in_specs=in_specs,
        out_specs=out_specs,
        scratch_shapes=scratch_shapes,
        name=name,
        compiler_params=pltpu.CompilerParams(vmem_limit_bytes=16 << 20),
        cost_estimate=pl.CostEstimate(flops=flops, bytes_accessed=1000, transcendentals=0),
        **kwargs,
    )


def body(echoes, steer_blocks, plan, filter_taps):
    pulses = lax.axis_size("pulse")
    others = pulses - 1
    subarrays, gates = echoes.shape[1], echoes.shape[3]
    blocks = gates // TILE
    span = filter_taps.shape[1] // TILE
    assert echoes.shape[2] == 1 and blocks == span and lax.axis_size("range") % 4 == 0
    cut = subarrays // 2
    left = subarrays - cut
    groups = ((0, cut), (cut, left))
    count = steer_blocks.shape[0] // plan.shape[1] * steer_blocks.shape[2]
    any_space = pl.BlockSpec(memory_space=pl.ANY)

    def shape(*dims, dtype=f32):
        return jax.ShapeDtypeStruct(dims, dtype)

    def halves(rows):
        return [pltpu.VMEM((blocks * rows, 2 * TILE), bf16)] * 2

    def spilling(rows):
        return [pltpu.VMEM((k * span * rows, 2 * TILE), bf16) for k in (1, 2)]

    out_shape = shape(2 * count, blocks, pulses, TILE)
    ya, yb = (pltpu.VMEM((6 * rows, gates), bf16) for rows in (cut, left))
    first = pltpu.VMEM((blocks * cut, 2 * TILE), f32)
    dense = [pltpu.VMEM((2 * count, gates), f32), pltpu.SemaphoreType.DMA((blocks,))]

    samples = echoes.reshape(2, subarrays, blocks, TILE)
    raw, rest = samples[:, :cut], samples[:, cut:]
    odd_rest = from_odd(rest)
    others_raw = [shifted(raw, "pulse", k) for k in range(1, pulses)]
    even = from_even(samples)
    odd_raw = from_odd(raw)

    th, tl, rest_partial = call(
        prepare_kernel,
        "prepare",
        [shape(span + 1, 2 * TILE, 2 * TILE, dtype=bf16)] * 2
        + [shape(blocks * left, 2 * TILE)],
        [VMEM] * 2,
        [VMEM] * 3,
        halves(left),
    )(filter_taps, rest)
    own_rest = call(
        functools.partial(rest_kernel, cut),
        "rest",
        shape(blocks * left, 2 * TILE),
        [VMEM] * 5,
        VMEM,
        spilling(left),
    )(even, odd_rest, rest_partial, th, tl)
    others_rest = [shifted(own_rest, "pulse", k) for k in range(1, pulses)]
    others_raw, own_rest = lax.optimization_barrier((others_raw, own_rest))

    def spilled(parity, raw, flops):
        return call(
            functools.partial(spill_kernel, parity),
            "spill",
            shape(span * cut, 2 * TILE),
            [VMEM, any_space, VMEM, VMEM],
            VMEM,
            spilling(cut),
            flops=flops,
        )(raw, own_rest, th, tl)

    odd_others = [from_odd(spilled(1, raw, LONG)) for raw in others_raw]
    even_others = [from_even(spilled(0, raw, SHORT)) for raw in others_raw]
    out, wa, wb, *partials = call(
        functools.partial(own_kernel, groups, others),
        "own",
        [out_shape]
        + [shape(2 * count, 6 * rows, dtype=bf16) for rows in (cut, left)]
        + [shape(blocks * cut, 2 * TILE)] * others,
        [VMEM] * (8 + others),
        [any_space] + [VMEM] * (2 + others),
        [
            *[first] * 2,
            *halves(cut),
            spilling(cut)[1],
            ya,
            yb,
            *dense,
            pltpu.VMEM((2 * subarrays, 2 * count), f32),
        ],
    )(
        plan.T,
        steer_blocks.transpose(0, 1, 3, 2),
        even,
        odd_raw,
        raw,
        own_rest,
        th,
        tl,
        *others_raw,
    )
    for k in range(1, pulses):
        ready = call(
            ready_kernel,
            "ready",
            shape(6 * left, gates, dtype=bf16),
            [VMEM],
            VMEM,
            [],
            flops=LONG >> 6,
        )(others_rest[k - 1])
        token = call(
            meet_kernel, "meet", shape(8, TILE), [any_space] * 2, VMEM, [], flops=LONG
        )(odd_others[k - 1], ready)
        out = call(
            functools.partial(other_kernel, k),
            "other",
            out_shape,
            [VMEM] * 6 + [any_space] * 2,
            any_space,
            [ya, *dense],
            input_output_aliases={7: 0},
        )(ready, even_others[k - 1], odd_others[k - 1], partials[k - 1], wa, wb, token, out)
    return out.transpose(0, 2, 1, 3).reshape(2, count, pulses, gates)


def solution(mesh):
    in_specs = (P(None, None, "pulse", "range"), P("pulse", None, None, None), P(), P())
    out_specs = P(None, "pulse", None, "range")
    return jax.shard_map(body, mesh=mesh, in_specs=in_specs, out_specs=out_specs, check_vma=False)
```

```python
import functools

import jax
import jax.numpy as jnp
from jax import lax
from jax.experimental import pallas as pl
from jax.experimental.pallas import tpu as pltpu
from jax.sharding import PartitionSpec as P

TILE = 128
f32 = jnp.float32
bf16 = jnp.bfloat16
VMEM = pl.BlockSpec(memory_space=pltpu.VMEM)
SHORT, LONG = 1000, 1 << 36


def dot(left, right):
    return jnp.dot(left, right, preferred_element_type=f32)


def split(value):
    high = value.astype(bf16)
    return high, (value - high.astype(f32)).astype(bf16)


def shifted(value, axis, steps):
    count = lax.axis_size(axis)
    return lax.ppermute(value, axis, [(i, (i + steps) % count) for i in range(count)])


def from_odd(value):
    count = lax.axis_size("range")
    target = {i: (i + 1) % count for i in range(count)}
    source, goal = count - 1, count - 5
    while goal > 0:
        target[source] = goal
        source, goal = goal - 1, goal - 4
    target[source] = 0
    return lax.ppermute(value, "range", list(target.items()))


def from_even(value):
    count = lax.axis_size("range")
    return lax.ppermute(value, "range", [(i, i ^ 1) for i in range(count)])


def make_tables(taps_ref, high_ref, low_ref):
    span = taps_ref.shape[1] // TILE
    row = lax.broadcasted_iota(jnp.int32, (TILE, TILE), 0)
    lane = lax.broadcasted_iota(jnp.int32, (TILE, TILE), 1)
    upper = lane >= row
    before = [jnp.zeros((TILE, TILE), f32)] * 2
    for offset in range(span + 1):
        for part in range(2):
            if offset < span:
                taps = taps_ref[part : part + 1, offset * TILE : (offset + 1) * TILE]
                rolled = pltpu.roll(
                    jnp.broadcast_to(taps, (TILE, TILE)), 0, 1, stride=1, stride_axis=0
                )
            else:
                rolled = jnp.zeros((TILE, TILE), f32)
            table = jnp.where(upper, rolled, before[part])
            before[part] = rolled
            high, low = split(table)
            for ref, value in ((high_ref, high), (low_ref, low)):
                if part == 0:
                    ref[offset, :TILE, :TILE] = value
                    ref[offset, TILE:, TILE:] = value
                else:
                    ref[offset, :TILE, TILE:] = value
                    ref[offset, TILE:, :TILE] = -value


def make_weights(plan_ref, steer_ref, outs, wide, groups):
    per_beam = plan_ref.shape[0]
    sub, width = steer_ref.shape[2:]
    beam_blocks = steer_ref.shape[0] // per_beam
    beams = beam_blocks * width
    first = lax.axis_index("pulse") * beam_blocks
    column = lax.broadcasted_iota(jnp.int32, plan_ref.shape, 1)
    for i in range(beam_blocks):
        mine = jnp.sum(jnp.where(column == first + i, plan_ref[...], 0), axis=1, keepdims=True)
        chosen = [mine[k : k + 1] for k in range(per_beam)]
        left = slice(i * width, (i + 1) * width)
        right = slice(beams + i * width, beams + (i + 1) * width)
        for at, size in groups:
            for start in range(at, at + size, sub):
                real = imag = jnp.zeros((sub, width), f32)
                for k in range(per_beam):
                    here = jnp.broadcast_to(chosen[k] == start // sub, (sub, width))
                    real = jnp.where(here, steer_ref[i * per_beam + k, 0], real)
                    imag = jnp.where(here, steer_ref[i * per_beam + k, 1], imag)
                re_row = at + start
                im_row = re_row + size
                wide[re_row : re_row + sub, left] = real
                wide[im_row : im_row + sub, left] = -imag
                wide[re_row : re_row + sub, right] = imag
                wide[im_row : im_row + sub, right] = real
    for ref, (at, size) in zip(outs, groups):
        high, low = split(wide[2 * at : 2 * (at + size), :].T)
        ref[...] = jnp.concatenate([high, high, low], axis=1)


def place(value, block, xh, xl, part):
    rows = value.shape[0]
    high, low = split(value)
    at = (slice(block * rows, (block + 1) * rows), slice(part * TILE, (part + 1) * TILE))
    xh[at] = high
    xl[at] = low


def product(xh, xl, at, high, low):
    return dot(xh[at, :], high) + dot(xl[at, :], high) + dot(xh[at, :], low)


def inner(own_ref, high_ref, low_ref, out_ref, xh, xl):
    rows, blocks = own_ref.shape[1:3]
    span = high_ref.shape[0] - 1
    for part in range(2):
        value = jnp.swapaxes(own_ref[part], 0, 1)
        for block in range(blocks):
            place(value[block], block, xh, xl, part)
    at = slice(0, blocks * rows)
    out_ref[...] = product(xh, xl, at, high_ref[0], low_ref[0])
    for offset in range(1, min(span + 1, blocks)):
        at = slice(0, (blocks - offset) * rows)
        out_ref[offset * rows :, :] += product(xh, xl, at, high_ref[offset], low_ref[offset])


def spill(values, high_ref, low_ref, out_ref, xh, both, given=None):
    span = high_ref.shape[0] - 1
    rows = xh.shape[0] // span
    for offset in range(1, span + 1):
        block = span - offset
        for part in range(2):
            high, low = split(values[part][block])
            lanes = slice(part * TILE, (part + 1) * TILE)
            xh[block * rows : (block + 1) * rows, lanes] = high
            both[2 * block * rows : (2 * block + 1) * rows, lanes] = high
            both[(2 * block + 1) * rows : (2 * block + 2) * rows, lanes] = low
        pair = dot(both[2 * block * rows :, :], high_ref[offset])
        rest = dot(xh[block * rows :, :], low_ref[offset])
        for target in range(offset):
            at = slice(target * rows, (target + 1) * rows)
            term = pair[2 * target * rows : (2 * target + 1) * rows, :] + rest[at, :]
            term = term + pair[(2 * target + 1) * rows : (2 * target + 2) * rows, :]
            if target < offset - 1:
                out_ref[at, :] += term
            elif given is None:
                out_ref[at, :] = term
            else:
                out_ref[at, :] = term + given[at, :]


def outer(even_ref, start, odd_ref, given, high_ref, low_ref, out_ref, xh, xl):
    rows = odd_ref.shape[1]
    index = lax.axis_index("range")

    @pl.when(index > 0)
    def _():
        values = []
        for part in range(2):
            value = even_ref[part, start : start + rows]
            value = jnp.where(lax.rem(index, 2) == 1, value, odd_ref[part])
            values.append(jnp.swapaxes(value, 0, 1))
        spill(values, high_ref, low_ref, out_ref, xh, xl, given)

    @pl.when(index == 0)
    def _():
        out_ref[...] = given[...]


def columns(ref, y, added=None):
    blocks = y.shape[1] // TILE
    rows = y.shape[0] // 6
    for block in range(blocks):
        lanes = slice(block * TILE, (block + 1) * TILE)
        at = slice(block * rows, (block + 1) * rows)
        total = ref[at, :] if added is None else ref[at, :] + added[at, :]
        for part in range(2):
            high, low = split(total[:, part * TILE : (part + 1) * TILE])
            for copy, value in enumerate((high, low, high)):
                base = (2 * copy + part) * rows
                y[base : base + rows, lanes] = value


def send(shift, dense, out_ref, start, stop, sems):
    pulses = out_ref.shape[2]
    pulse = lax.rem(lax.axis_index("pulse") + pulses - shift, pulses)
    copies = []
    for block in range(start, stop):
        copy = pltpu.make_async_copy(
            dense.at[:, block * TILE : (block + 1) * TILE],
            out_ref.at[:, block, pulse, :],
            sems.at[block],
        )
        copy.start()
        copies.append(copy)
    return copies


def parts_of(blocks):
    half = -(-blocks // 2)
    return [(0, half), (half, blocks)] if half < blocks else [(0, blocks)]


def prepare_kernel(taps, rest, th, tl, partial, xh, xl):
    make_tables(taps, th, tl)
    inner(rest, th, tl, partial, xh, xl)


def rest_kernel(cut, even, odd, partial, th, tl, out, xh, xl):
    outer(even, cut, odd, partial, th, tl, out, xh, xl)


def own_kernel(groups, others, plan, steer, even, odd, own, rest, th, tl, *refs):
    raws, (out, wa, wb), partials = refs[:others], refs[others : others + 3], refs[others + 3 : 2 * others + 3]
    whole, first, xh, xl, both, ya, yb, dense, sems, wide = refs[2 * others + 3 :]
    make_weights(plan, steer, (wa, wb), wide, groups)
    columns(rest, yb)
    inner(own, th, tl, whole, xh, xl)
    outer(even, 0, odd, whole, th, tl, first, xh, both)
    columns(first, ya)
    copies = []
    for start, stop in parts_of(out.shape[1]):
        lanes = slice(start * TILE, stop * TILE)
        dense[:, lanes] = dot(wa[...], ya[:, lanes]) + dot(wb[...], yb[:, lanes])
        copies += send(0, dense, out, start, stop, sems)
    for raw, result in zip(raws, partials):
        inner(raw, th, tl, result, xh, xl)
    for copy in copies:
        copy.wait()


def spill_kernel(parity, own, after, th, tl, out, xh, xl):
    span = th.shape[0] - 1

    @pl.when(lax.rem(lax.axis_index("range"), 2) == parity)
    def _():
        values = [jnp.swapaxes(own[part, :, own.shape[2] - span :], 0, 1) for part in range(2)]
        spill(values, th, tl, out, xh, xl)


def ready_kernel(rest, wb, out, yb):
    columns(rest, yb)
    out[...] = dot(wb[...], yb[...])


def meet_kernel(odd, yb, token):
    token[...] = jnp.zeros_like(token)


def other_kernel(shift, part, even, odd, partial, wa, token, held, out, ya, dense, sems):
    index = lax.axis_index("range")
    spilled = jnp.where(lax.rem(index, 2) == 1, even[...], odd[...])
    columns(partial, ya, jnp.where(index == 0, 0.0, spilled))
    dense[...] = dot(wa[...], ya[...]) + part[...]
    for copy in send(shift, dense, out, 0, out.shape[1], sems):
        copy.wait()


def call(kernel, name, out_shape, in_specs, out_specs, scratch_shapes, flops=SHORT, **kwargs):
    return pl.pallas_call(
        kernel,
        out_shape=out_shape,
        in_specs=in_specs,
        out_specs=out_specs,
        scratch_shapes=scratch_shapes,
        name=name,
        compiler_params=pltpu.CompilerParams(vmem_limit_bytes=16 << 20),
        cost_estimate=pl.CostEstimate(flops=flops, bytes_accessed=1000, transcendentals=0),
        **kwargs,
    )


def body(echoes, steer_blocks, plan, filter_taps):
    pulses = lax.axis_size("pulse")
    others = pulses - 1
    subarrays, gates = echoes.shape[1], echoes.shape[3]
    blocks = gates // TILE
    span = filter_taps.shape[1] // TILE
    assert echoes.shape[2] == 1 and blocks == span and lax.axis_size("range") % 4 == 0
    cut = subarrays // 2
    left = subarrays - cut
    groups = ((0, cut), (cut, left))
    count = steer_blocks.shape[0] // plan.shape[1] * steer_blocks.shape[2]
    any_space = pl.BlockSpec(memory_space=pl.ANY)

    def shape(*dims, dtype=f32):
        return jax.ShapeDtypeStruct(dims, dtype)

    def halves(rows):
        return [pltpu.VMEM((blocks * rows, 2 * TILE), bf16)] * 2

    def spilling(rows):
        return [pltpu.VMEM((k * span * rows, 2 * TILE), bf16) for k in (1, 2)]

    out_shape = shape(2 * count, blocks, pulses, TILE)
    ya, yb = (pltpu.VMEM((6 * rows, gates), bf16) for rows in (cut, left))
    first = pltpu.VMEM((blocks * cut, 2 * TILE), f32)
    dense = [pltpu.VMEM((2 * count, gates), f32), pltpu.SemaphoreType.DMA((blocks,))]

    samples = echoes.reshape(2, subarrays, blocks, TILE)
    raw, rest = samples[:, :cut], samples[:, cut:]
    odd_rest = from_odd(rest)
    others_raw = [shifted(raw, "pulse", k) for k in range(1, pulses)]
    even = from_even(samples)
    odd_raw = from_odd(raw)

    th, tl, rest_partial = call(
        prepare_kernel,
        "prepare",
        [shape(span + 1, 2 * TILE, 2 * TILE, dtype=bf16)] * 2
        + [shape(blocks * left, 2 * TILE)],
        [VMEM] * 2,
        [VMEM] * 3,
        halves(left),
    )(filter_taps, rest)
    own_rest = call(
        functools.partial(rest_kernel, cut),
        "rest",
        shape(blocks * left, 2 * TILE),
        [VMEM] * 5,
        VMEM,
        spilling(left),
    )(even, odd_rest, rest_partial, th, tl)
    others_rest = [shifted(own_rest, "pulse", k) for k in range(1, pulses)]
    others_raw, own_rest = lax.optimization_barrier((others_raw, own_rest))

    def spilled(parity, raw, flops):
        return call(
            functools.partial(spill_kernel, parity),
            "spill",
            shape(span * cut, 2 * TILE),
            [VMEM, any_space, VMEM, VMEM],
            VMEM,
            spilling(cut),
            flops=flops,
        )(raw, own_rest, th, tl)

    odd_others = [from_odd(spilled(1, raw, LONG)) for raw in others_raw]
    even_others = [from_even(spilled(0, raw, SHORT)) for raw in others_raw]
    out, wa, wb, *partials = call(
        functools.partial(own_kernel, groups, others),
        "own",
        [out_shape]
        + [shape(2 * count, 6 * rows, dtype=bf16) for rows in (cut, left)]
        + [shape(blocks * cut, 2 * TILE)] * others,
        [VMEM] * (8 + others),
        [any_space] + [VMEM] * (2 + others),
        [
            *[first] * 2,
            *halves(cut),
            spilling(cut)[1],
            ya,
            yb,
            *dense,
            pltpu.VMEM((2 * subarrays, 2 * count), f32),
        ],
    )(
        plan.T,
        steer_blocks.transpose(0, 1, 3, 2),
        even,
        odd_raw,
        raw,
        own_rest,
        th,
        tl,
        *others_raw,
    )
    for k in range(1, pulses):
        ready = call(
            ready_kernel,
            "ready",
            shape(2 * count, gates),
            [VMEM] * 2,
            VMEM,
            [yb],
            flops=LONG >> 6,
        )(others_rest[k - 1], wb)
        token = call(
            meet_kernel, "meet", shape(8, TILE), [any_space] * 2, VMEM, [], flops=LONG
        )(odd_others[k - 1], ready)
        out = call(
            functools.partial(other_kernel, k),
            "other",
            out_shape,
            [VMEM] * 5 + [any_space] * 2,
            any_space,
            [ya, *dense],
            input_output_aliases={6: 0},
        )(ready, even_others[k - 1], odd_others[k - 1], partials[k - 1], wa, token, out)
    return out.transpose(0, 2, 1, 3).reshape(2, count, pulses, gates)


def solution(mesh):
    in_specs = (P(None, None, "pulse", "range"), P("pulse", None, None, None), P(), P())
    out_specs = P(None, "pulse", None, "range")
    return jax.shard_map(body, mesh=mesh, in_specs=in_specs, out_specs=out_specs, check_vma=False)
```

```python
import functools

import jax
import jax.numpy as jnp
from jax import lax
from jax.experimental import pallas as pl
from jax.experimental.pallas import tpu as pltpu
from jax.sharding import PartitionSpec as P

TILE = 128
f32 = jnp.float32
bf16 = jnp.bfloat16
VMEM = pl.BlockSpec(memory_space=pltpu.VMEM)
SMEM = pl.BlockSpec(memory_space=pltpu.SMEM)


def dot(left, right):
    return jnp.dot(left, right, preferred_element_type=f32)


def split(value):
    high = value.astype(bf16)
    return high, (value - high.astype(f32)).astype(bf16)


def shifted(value, axis, steps):
    count = lax.axis_size(axis)
    return lax.ppermute(value, axis, [(i, (i + steps) % count) for i in range(count)])


def from_odd(value):
    count = lax.axis_size("range")
    target = {i: (i + 1) % count for i in range(count)}
    source, goal = count - 1, count - 5
    while goal > 0:
        target[source] = goal
        source, goal = goal - 1, goal - 4
    target[source] = 0
    return lax.ppermute(value, "range", list(target.items()))


def from_even(value):
    count = lax.axis_size("range")
    return lax.ppermute(value, "range", [(i, i ^ 1) for i in range(count)])


def make_tables(taps_ref, high_ref, low_ref):
    span = taps_ref.shape[1] // TILE
    row = lax.broadcasted_iota(jnp.int32, (TILE, TILE), 0)
    lane = lax.broadcasted_iota(jnp.int32, (TILE, TILE), 1)
    upper = lane >= row
    before = [jnp.zeros((TILE, TILE), f32)] * 2
    for offset in range(span + 1):
        for part in range(2):
            if offset < span:
                taps = taps_ref[part : part + 1, offset * TILE : (offset + 1) * TILE]
                rolled = pltpu.roll(
                    jnp.broadcast_to(taps, (TILE, TILE)), 0, 1, stride=1, stride_axis=0
                )
            else:
                rolled = jnp.zeros((TILE, TILE), f32)
            table = jnp.where(upper, rolled, before[part])
            before[part] = rolled
            high, low = split(table)
            for ref, value in ((high_ref, high), (low_ref, low)):
                if part == 0:
                    ref[offset, :TILE, :TILE] = value
                    ref[offset, TILE:, TILE:] = value
                else:
                    ref[offset, :TILE, TILE:] = value
                    ref[offset, TILE:, :TILE] = -value


def make_weights(plan_ref, steer_ref, outs, wide, groups):
    per_beam = plan_ref.shape[0]
    sub, width = steer_ref.shape[2:]
    beam_blocks = steer_ref.shape[0] // per_beam
    beams = beam_blocks * width
    first = lax.axis_index("pulse") * beam_blocks
    column = lax.broadcasted_iota(jnp.int32, plan_ref.shape, 1)
    for i in range(beam_blocks):
        mine = jnp.sum(jnp.where(column == first + i, plan_ref[...], 0), axis=1, keepdims=True)
        chosen = [mine[k : k + 1] for k in range(per_beam)]
        left = slice(i * width, (i + 1) * width)
        right = slice(beams + i * width, beams + (i + 1) * width)
        for at, size in groups:
            for start in range(at, at + size, sub):
                real = imag = jnp.zeros((sub, width), f32)
                for k in range(per_beam):
                    here = jnp.broadcast_to(chosen[k] == start // sub, (sub, width))
                    real = jnp.where(here, steer_ref[i * per_beam + k, 0], real)
                    imag = jnp.where(here, steer_ref[i * per_beam + k, 1], imag)
                re_row = at + start
                im_row = re_row + size
                wide[re_row : re_row + sub, left] = real
                wide[im_row : im_row + sub, left] = -imag
                wide[re_row : re_row + sub, right] = imag
                wide[im_row : im_row + sub, right] = real
    for ref, (at, size) in zip(outs, groups):
        high, low = split(wide[2 * at : 2 * (at + size), :].T)
        ref[...] = jnp.concatenate([high, high, low], axis=1)


def place(value, block, xh, xl, part):
    rows = value.shape[0]
    high, low = split(value)
    at = (slice(block * rows, (block + 1) * rows), slice(part * TILE, (part + 1) * TILE))
    xh[at] = high
    xl[at] = low


def product(xh, xl, at, high, low):
    return dot(xh[at, :], high) + dot(xl[at, :], high) + dot(xh[at, :], low)


def inner(own_ref, high_ref, low_ref, out_ref, xh, xl):
    rows, blocks = own_ref.shape[1:3]
    span = high_ref.shape[0] - 1
    for part in range(2):
        value = jnp.swapaxes(own_ref[part], 0, 1)
        for block in range(blocks):
            place(value[block], block, xh, xl, part)
    at = slice(0, blocks * rows)
    out_ref[...] = product(xh, xl, at, high_ref[0], low_ref[0])
    for offset in range(1, min(span + 1, blocks)):
        at = slice(0, (blocks - offset) * rows)
        out_ref[offset * rows :, :] += product(xh, xl, at, high_ref[offset], low_ref[offset])


def spill(values, high_ref, low_ref, out_ref, xh, both, given=None):
    span = high_ref.shape[0] - 1
    rows = xh.shape[0] // span
    for offset in range(1, span + 1):
        block = span - offset
        for part in range(2):
            high, low = split(values[part][block])
            lanes = slice(part * TILE, (part + 1) * TILE)
            xh[block * rows : (block + 1) * rows, lanes] = high
            both[2 * block * rows : (2 * block + 1) * rows, lanes] = high
            both[(2 * block + 1) * rows : (2 * block + 2) * rows, lanes] = low
        pair = dot(both[2 * block * rows :, :], high_ref[offset])
        rest = dot(xh[block * rows :, :], low_ref[offset])
        for target in range(offset):
            at = slice(target * rows, (target + 1) * rows)
            term = pair[2 * target * rows : (2 * target + 1) * rows, :] + rest[at, :]
            term = term + pair[(2 * target + 1) * rows : (2 * target + 2) * rows, :]
            if target < offset - 1:
                out_ref[at, :] += term
            elif given is None:
                out_ref[at, :] = term
            else:
                out_ref[at, :] = term + given[at, :]


def outer(even_ref, start, odd_ref, given, high_ref, low_ref, out_ref, xh, xl):
    rows = odd_ref.shape[1]
    index = lax.axis_index("range")

    @pl.when(index > 0)
    def _():
        values = []
        for part in range(2):
            value = even_ref[part, start : start + rows]
            value = jnp.where(lax.rem(index, 2) == 1, value, odd_ref[part])
            values.append(jnp.swapaxes(value, 0, 1))
        spill(values, high_ref, low_ref, out_ref, xh, xl, given)

    @pl.when(index == 0)
    def _():
        out_ref[...] = given[...]


def columns(ref, y):
    blocks = y.shape[1] // TILE
    rows = y.shape[0] // 6
    for block in range(blocks):
        lanes = slice(block * TILE, (block + 1) * TILE)
        for part in range(2):
            high, low = split(ref[block * rows : (block + 1) * rows, part * TILE : (part + 1) * TILE])
            for copy, value in enumerate((high, low, high)):
                base = (2 * copy + part) * rows
                y[base : base + rows, lanes] = value


def send(shift, dense, out_ref, start, stop, sems):
    pulses = out_ref.shape[2]
    pulse = lax.rem(lax.axis_index("pulse") + pulses - shift, pulses)
    copies = []
    for block in range(start, stop):
        copy = pltpu.make_async_copy(
            dense.at[:, block * TILE : (block + 1) * TILE],
            out_ref.at[:, block, pulse, :],
            sems.at[block],
        )
        copy.start()
        copies.append(copy)
    return copies


def parts_of(blocks):
    half = -(-blocks // 2)
    return [(0, half), (half, blocks)] if half < blocks else [(0, blocks)]


def prepare_kernel(taps, rest, th, tl, rest_partial, *scratch):
    make_tables(taps, th, tl)
    inner(rest, th, tl, rest_partial, *scratch[:2])


def rest_kernel(cut, even, odd, partial, th, tl, out, xh, xl):
    outer(even, cut, odd, partial, th, tl, out, xh, xl)


def own_kernel(groups, others, plan, steer, even, odd, own, rest, th, tl, *refs):
    raws, (out, wa, wb), partials = refs[:others], refs[others : others + 3], refs[others + 3 : 2 * others + 3]
    whole, first, xh, xl, both, ya, yb, dense, sems, wide = refs[2 * others + 3 :]
    make_weights(plan, steer, (wa, wb), wide, groups)
    columns(rest, yb)
    inner(own, th, tl, whole, xh, xl)
    outer(even, 0, odd, whole, th, tl, first, xh, both)
    columns(first, ya)
    copies = []
    for start, stop in parts_of(out.shape[1]):
        lanes = slice(start * TILE, stop * TILE)
        dense[:, lanes] = dot(wa[...], ya[:, lanes]) + dot(wb[...], yb[:, lanes])
        copies += send(0, dense, out, start, stop, sems)
    for raw, result in zip(raws, partials):
        inner(raw, th, tl, result, xh, xl)
    for copy in copies:
        copy.wait()


def spill_kernel(parity, own, after, th, tl, out, xh, xl):
    span = th.shape[0] - 1

    @pl.when(lax.rem(lax.axis_index("range"), 2) == parity)
    def _():
        values = [jnp.swapaxes(own[part, :, own.shape[2] - span :], 0, 1) for part in range(2)]
        spill(values, th, tl, out, xh, xl)


def ready_kernel(rest, yb):
    columns(rest, yb)


def meet_kernel(odd, yb, token):
    token[...] = jnp.zeros_like(token)


def other_kernel(shift, yb, even, odd, partial, wa, wb, token, held, out, first, ya, dense, sems):
    index = lax.axis_index("range")
    count = even.shape[0]
    spilled = jnp.where(lax.rem(index, 2) == 1, even[...], odd[:count, :])
    spilled = jnp.where(index == 0, 0.0, spilled)
    first[...] = partial[...]
    first[:count, :] += spilled
    columns(first, ya)
    copies = []
    for start, stop in [(0, out.shape[1])]:
        lanes = slice(start * TILE, stop * TILE)
        dense[:, lanes] = dot(wa[...], ya[:, lanes]) + dot(wb[...], yb[:, lanes])
        copies += send(shift, dense, out, start, stop, sems)
    for copy in copies:
        copy.wait()


def call(kernel, name, out_shape, in_specs, out_specs, scratch_shapes, flops=1000, **kwargs):
    return pl.pallas_call(
        kernel,
        out_shape=out_shape,
        in_specs=in_specs,
        out_specs=out_specs,
        scratch_shapes=scratch_shapes,
        name=name,
        compiler_params=pltpu.CompilerParams(vmem_limit_bytes=16 << 20),
        cost_estimate=pl.CostEstimate(flops=flops, bytes_accessed=1000, transcendentals=0),
        **kwargs,
    )


def body(echoes, steer_blocks, plan, filter_taps):
    pulses = lax.axis_size("pulse")
    others = pulses - 1
    subarrays, gates = echoes.shape[1], echoes.shape[3]
    blocks = gates // TILE
    span = filter_taps.shape[1] // TILE
    assert echoes.shape[2] == 1 and blocks == span and lax.axis_size("range") % 4 == 0
    cut = subarrays // 2
    left = subarrays - cut
    groups = ((0, cut), (cut, left))
    count = steer_blocks.shape[0] // plan.shape[1] * steer_blocks.shape[2]
    any_space = pl.BlockSpec(memory_space=pl.ANY)

    def shape(*dims, dtype=f32):
        return jax.ShapeDtypeStruct(dims, dtype)

    def halves(rows):
        return [pltpu.VMEM((blocks * rows, 2 * TILE), bf16)] * 2

    def spilling(rows):
        return [pltpu.VMEM((k * span * rows, 2 * TILE), bf16) for k in (1, 2)]

    out_shape = shape(2 * count, blocks, pulses, TILE)
    ya, yb = (pltpu.VMEM((6 * rows, gates), bf16) for rows in (cut, left))
    first = pltpu.VMEM((blocks * cut, 2 * TILE), f32)
    dense = [pltpu.VMEM((2 * count, gates), f32), pltpu.SemaphoreType.DMA((blocks,))]

    samples = echoes.reshape(2, subarrays, blocks, TILE)
    tail = slice(blocks - span, blocks)
    raw, rest = samples[:, :cut], samples[:, cut:]
    odd_rest = from_odd(rest[:, :, tail])
    others_raw = [shifted(raw, "pulse", k) for k in range(1, pulses)]
    samples, raw, rest = lax.optimization_barrier((samples, raw, rest))
    even = from_even(samples[:, :, tail])
    odd_raw = from_odd(raw[:, :, tail])

    th, tl, rest_partial = call(
        prepare_kernel,
        "prepare",
        [shape(span + 1, 2 * TILE, 2 * TILE, dtype=bf16)] * 2
        + [shape(blocks * left, 2 * TILE)],
        [VMEM] * 2,
        [VMEM] * 3,
        halves(left),
    )(filter_taps, rest)
    own_rest = call(
        functools.partial(rest_kernel, cut),
        "rest",
        shape(blocks * left, 2 * TILE),
        [VMEM] * 5,
        VMEM,
        spilling(left),
    )(even, odd_rest, rest_partial, th, tl)
    others_rest = [shifted(own_rest, "pulse", k) for k in range(1, pulses)]
    others_raw, own_rest = lax.optimization_barrier((others_raw, own_rest))
    def spilled(parity, raw, flops, more):
        return call(
            functools.partial(spill_kernel, parity),
            "spill",
            shape(span * cut + more, 2 * TILE),
            [VMEM, any_space, VMEM, VMEM],
            VMEM,
            spilling(cut),
            flops=flops,
        )(raw, own_rest, th, tl)

    odd_others = [from_odd(spilled(1, raw, 1 << 36, 0)) for raw in others_raw]
    even_others = [from_even(spilled(0, raw, 1000, 0)) for raw in others_raw]
    out, wa, wb, *partials = call(
        functools.partial(own_kernel, groups, others),
        "own",
        [out_shape]
        + [shape(2 * count, 6 * rows, dtype=bf16) for rows in (cut, left)]
        + [shape(blocks * cut, 2 * TILE)] * others,
        [VMEM] * (8 + others),
        [any_space] + [VMEM] * (2 + others),
        [first, first, *halves(cut), spilling(cut)[1], ya, yb, *dense, pltpu.VMEM((2 * subarrays, 2 * count), f32)],
    )(
        plan.T,
        steer_blocks.transpose(0, 1, 3, 2),
        even,
        odd_raw,
        raw,
        own_rest,
        th,
        tl,
        *others_raw,
    )
    for k in range(1, pulses):
        ready = call(
            ready_kernel,
            "ready",
            shape(6 * left, gates, dtype=bf16),
            [VMEM],
            VMEM,
            [],
            flops=1 << 30,
        )(others_rest[k - 1])
        token = call(
            meet_kernel, "meet", shape(8, TILE), [any_space] * 2, VMEM, [], flops=1 << 36
        )(odd_others[k - 1], ready)
        out = call(
            functools.partial(other_kernel, k),
            "other",
            out_shape,
            [VMEM] * 6 + [any_space] * 2,
            any_space,
            [first, ya, *dense],
            input_output_aliases={7: 0},
        )(ready, even_others[k - 1], odd_others[k - 1], partials[k - 1], wa, wb, token, out)
    return out.transpose(0, 2, 1, 3).reshape(2, count, pulses, gates)


def solution(mesh):
    in_specs = (P(None, None, "pulse", "range"), P("pulse", None, None, None), P(), P())
    out_specs = P(None, "pulse", None, "range")
    return jax.shard_map(body, mesh=mesh, in_specs=in_specs, out_specs=out_specs, check_vma=False)
```
